128 devices in a mesh: section: 4 (over x_hi, core), expert: 32 (over x_lo, z, y).
Axes of the slice: x: 4 (x_hi: 2, x_lo: 2; x = x_hi * 2 + x_lo), y: 4, z: 4, core: 2. Of those that a mesh axis runs over, the one named last changes fastest.
Arguments:
- batches: bfloat16 [4, 2048, 3584], P(None, 'expert'), may hold values from -6 to 6
- order: int32 [4], replicated, may hold values from 0 to 3, each once
- gains: float32 [4, 3584], P('section'), may hold values from 0.25 to 1.75
- router: float32 [4, 3584, 8], P('section'), may hold values from -0.09375 to 0.09375
- routes: int32 [4, 2, 2048, 2], P('section', None, 'expert'), may hold values from 0 to 7, all different within a row; in each aligned block of 64 rows (0 to 63, 64 to 127, ..., all dimensions but the last counted through in order) at most 18 rows name the same one
- caps: int32 [4, 8], P('section'), may hold values from 9 to 18, as said below
- w_in: bfloat16 [4, 2, 3584, 16384], P('section', None, None, 'expert'), may hold values from -0.09375 to 0.09375
- w_down: bfloat16 [4, 16384, 3584], P('section', 'expert'), may hold values from -0.125 to 0.125
Outputs:
- acts: bfloat16 [4, 2, 2048, 3584], P('section', None, 'expert')
The draws below stay inside these ranges and needn't reach their ends.
Inputs may be any that keep to these rules, and one draw needn't show every extreme that they name: `caps`: each layer has at least one expert of capacity exactly 18. `routes`: no expert is named by more than 18 pairs among the tokens of one index of expert.
All inputs are finite; a program needn't handle non-finite values.
Results may differ from the reference program's by a relative error of at most 0.028.
Values may be sent and summed in bfloat16 or wider, within the bound.
A program may use at most 128 MiB of HBM per device.

```python
import math
import jax
import jax.numpy as jnp
import numpy as np
from jax import lax

D = 3584
FFE = 2048
EXPERTS = 8
TOPK = 2
BATCHES = 4
TOK_DEV = 64
CAP = 18
LAYERS = 4
TOKENS = 2048
N_EXPERT = 32


def draw_caps(key, part):
    key = jax.random.fold_in(key, 7)
    first, second = jax.random.split(key)
    values = jax.random.randint(first, (LAYERS, EXPERTS), CAP // 2, CAP + 1)
    where_full = jax.random.randint(second, (LAYERS, 1), 0, EXPERTS)
    full = where_full == jnp.arange(EXPERTS, dtype=jnp.int32)[None, :]
    return jnp.where(full, CAP, values).astype(jnp.int32)


def block_levels(own_key, shape, cuts, low, top_value):
    level, own = 1.0, jax.random.fold_in(own_key, 6)
    for axis_at, shards_of in cuts:
        steps = jnp.exp(jax.random.uniform(jax.random.fold_in(own, axis_at), (shards_of,), jnp.float32, low / len(cuts), top_value / len(cuts)))
        level = level * jnp.repeat(steps, shape[axis_at] // shards_of).reshape([-1 if axis == axis_at else 1 for axis in range(len(shape))])
    return level


def assign_block(own_key, own, number, rows, number_of, top, reach, skew):
    sequence = jax.random.permutation(own_key, number_of)
    packed, usual = shares(number_of, rows * top, reach, skew, True), shares(number_of, rows * top, reach, skew, False)
    places = jnp.arange(number_of)

    def named(sizes, offset_by):
        used = int((sizes > 0).sum())
        fixed = max(1, used // 4)
        shifted = fixed + (places - fixed + offset_by * (used - fixed)) % max(1, number_of - fixed)
        return jnp.zeros((number_of,), jnp.int32).at[sequence[jnp.where(places < fixed, places, shifted)]].set(jnp.asarray(sizes, jnp.int32))

    sizes = jnp.where(number % 4 == 0, named(packed, number // 4), named(usual, number - number // 4 - 1))
    mixed = jax.random.permutation(jax.random.fold_in(own, 3), number_of)
    donor, taker = mixed[0:number_of // 2 * 2:2], mixed[1:number_of // 2 * 2:2]
    margin = jnp.minimum(sizes[donor] - 1, reach - sizes[taker]) // 2
    margin = jnp.where((donor == sequence[0]) | (taker == sequence[0]) | (sizes[taker] == 0), 0, jnp.maximum(margin, 0))
    shifted = jax.random.randint(jax.random.fold_in(own, 4), (number_of // 2,), 0, 1 << 20) % (margin + 1)
    sizes = sizes.at[donor].add(-shifted).at[taker].add(shifted)
    members = jnp.searchsorted(jnp.cumsum(sizes), jnp.arange(rows * top), side="right").astype(jnp.int32)
    table = members.reshape(top, rows).T
    table = table[jax.random.permutation(jax.random.fold_in(own, 1), rows)]
    offset_by = jax.random.randint(jax.random.fold_in(own, 2), (rows, 1), 0, top)
    return jnp.take_along_axis(table, (jnp.arange(top)[None, :] + offset_by) % top, axis=1)


def shares(amount, total, reach, slope, full):
    portions = [(1 << 20) // math.isqrt(grade ** slope) + 1 for grade in range(1, amount + 1)]
    largest = reach if full else min(reach, max(-(-total // amount), total * portions[0] // sum(portions)))
    least = 1 if total - largest >= amount - 1 else 0
    given, spare = [largest] + [least] * (amount - 1), total - largest - least * (amount - 1)
    while spare > 0:
        free = [i for i in range(1, amount) if given[i] < largest] or [i for i in range(1, amount) if given[i] < reach]
        pool, left = sum([portions[i] for i in free]), spare
        for i in free:
            extra = min(reach - given[i], max(1, left * portions[i] // pool), spare)
            given[i] = given[i] + extra
            spare = spare - extra
    return np.array(given)


def noise(own_key, extent, spread, most, cuts=(), kind=jnp.bfloat16):
    array = spread * jax.random.normal(own_key, extent, jnp.float32)
    if cuts:
        array = array * block_levels(own_key, extent, cuts, -0.22, 0.18)
    return jnp.clip(array, -most, most).astype(kind)


def setup_inputs(seed: int = 0) -> dict:
    splits = jax.random.split(jax.random.key(seed), 9)
    batches = noise(splits[0], (BATCHES, TOKENS, D), 1.0, 6.0, ((1, 32),))
    order = jax.random.permutation(splits[1], BATCHES).astype(jnp.int32)
    gains = jnp.clip(1.0 + 0.15 * jax.random.normal(splits[2], (LAYERS, D), jnp.float32), 0.25, 1.75)
    router = noise(splits[3], (LAYERS, D, EXPERTS), D ** -0.5, 0.09375, ((0, 4),), jnp.float32)
    routes_keys = jax.random.split(jax.random.fold_in(splits[4], 1), LAYERS * 2 * TOKENS // TOK_DEV)
    routes_turns = jax.random.permutation(jax.random.fold_in(splits[4], 3), LAYERS * 2 * TOKENS // TOK_DEV)
    routes = jax.vmap(lambda own, number: assign_block(jax.random.fold_in(splits[4], 2), own, number, TOK_DEV, EXPERTS, TOPK, CAP, 2))(routes_keys, routes_turns).reshape((LAYERS, 2, TOKENS, TOPK))
    caps = draw_caps(jax.random.fold_in(splits[8], 71), 0)
    w_in = noise(splits[6], (LAYERS, 2, D, EXPERTS * FFE), D ** -0.5, 0.09375, ((0, 4), (3, 32)))
    w_down = noise(splits[7], (LAYERS, EXPERTS * FFE, D), FFE ** -0.5, 0.125, ((0, 4), (1, 32)))
    return {"batches": batches, "order": order, "gains": gains, "router": router, "routes": routes, "caps": caps, "w_in": w_in, "w_down": w_down}


def layer(tokens_in, gain, router_w, cap_row, route_row, gate_up, down):
    x32 = tokens_in.astype(jnp.float32)
    normed = (x32 * lax.rsqrt(lax.optimization_barrier(jnp.mean(x32 * x32, axis=-1, keepdims=True)) + 1e-06) * gain).astype(jnp.bfloat16)
    logits = jnp.dot(normed.astype(jnp.float32), router_w, precision=lax.Precision.HIGHEST)
    scores = jax.nn.sigmoid(logits)
    chosen = jnp.take_along_axis(scores, route_row, axis=1)
    gates = 2.5 * chosen / lax.optimization_barrier(jnp.sum(chosen, axis=1, keepdims=True))
    flat = route_row.reshape(N_EXPERT, TOK_DEV * TOPK)
    onehot = (flat[:, :, None] == jnp.arange(EXPERTS, dtype=jnp.int32)[None, None, :]).astype(jnp.int32)
    ranks = lax.optimization_barrier(jnp.sum((jnp.cumsum(onehot, axis=1) - onehot) * onehot, axis=-1)).astype(jnp.int32)
    kept = ranks < cap_row[flat]
    slots = jnp.where(kept, flat * CAP + ranks, EXPERTS * CAP).astype(jnp.int32)
    rows = jnp.repeat(normed.reshape(N_EXPERT, TOK_DEV, D), TOPK, axis=1)
    buffer = jnp.zeros((N_EXPERT, EXPERTS * CAP + 1, D), jnp.bfloat16)
    buffer = buffer.at[jnp.arange(N_EXPERT, dtype=jnp.int32)[:, None], slots].set(rows)
    buffer = buffer[:, :EXPERTS * CAP].reshape(N_EXPERT, EXPERTS, CAP, D)
    per_expert = jnp.transpose(buffer, (1, 0, 2, 3)).reshape(EXPERTS, N_EXPERT * CAP, D)
    pieces = N_EXPERT // EXPERTS
    width = FFE // pieces

    def expert(index):
        rows_e = per_expert[index]
        w_e = lax.dynamic_slice_in_dim(gate_up, index * FFE, FFE, 2)
        both = jnp.einsum('rd,gdf->grf', rows_e.astype(jnp.float32), w_e.astype(jnp.float32), precision=lax.Precision.HIGHEST)
        hidden = (jax.nn.silu(both[0]) * both[1]).astype(jnp.bfloat16)
        w_d = lax.dynamic_slice_in_dim(down, index * FFE, FFE, 0).reshape(pieces, width, D)
        parts = jnp.einsum('rsf,sfd->srd', hidden.reshape(-1, pieces, width).astype(jnp.float32), w_d.astype(jnp.float32), precision=lax.Precision.HIGHEST).astype(jnp.bfloat16)
        return lax.optimization_barrier(jnp.sum(parts.astype(jnp.float32), axis=0))
    outs = lax.map(expert, jnp.arange(EXPERTS, dtype=jnp.int32))
    outs = jnp.transpose(outs.reshape(EXPERTS, N_EXPERT, CAP, D), (1, 0, 2, 3)).reshape(N_EXPERT, EXPERTS * CAP, D)
    picked = jnp.take_along_axis(outs, jnp.where(kept, slots, 0)[:, :, None], axis=1)
    weight = gates.reshape(N_EXPERT, TOK_DEV * TOPK) * kept.astype(jnp.float32)
    moe = lax.optimization_barrier(jnp.sum((picked * weight[:, :, None]).reshape(TOKENS, TOPK, D), axis=1))
    return (x32 + moe).astype(jnp.bfloat16)

def reference(batches, order, gains, router, routes, caps, w_in, w_down):
    results = [[None, None] for level in range(LAYERS)]
    for direction in range(2):
        current = jnp.take(batches, order[direction], axis=0)
        levels = list(range(LAYERS)) if direction == 0 else list(range(LAYERS - 1, -1, -1))
        for level in levels:
            current = layer(current, gains[level], router[level], caps[level], routes[level, direction], w_in[level], w_down[level])
            results[level][direction] = current
    return jnp.stack([jnp.stack(pair) for pair in results])
```

```python
import jax
import jax.numpy as jnp
from jax import lax
from jax.experimental import pallas as pl
from jax.experimental.pallas import tpu as pltpu
from jax.sharding import PartitionSpec as P

MESH = pl.DeviceIdType.MESH
BF, F32, I32 = jnp.bfloat16, jnp.float32, jnp.int32

D = 3584
EXPERTS = 8
HALF = D // 2
BLK = 256
NBLK = HALF // BLK
WIDE = HALF + BLK
TOK = 64
HID = 512
ROWS = 256
XROWS = 288
LOST = 99.0


def iota(shape, dim):
    return lax.broadcasted_iota(I32, shape, dim)


def nt(a, b):
    return lax.dot_general(a, b, (((1,), (1,)), ((), ())), preferred_element_type=F32)


def mm(a, b):
    return jnp.dot(a, b, preferred_element_type=F32)


def kernel(
    order_ref, batches_ref, gain_ref, router_ref, routes_ref, caps_ref, w_in_hbm, w_down_hbm, out_ref,
    w_in, w_down, u_buf, normed, onehot, rk, gates, sel, pack,
    nb, x_buf, sa, sb, hidden, ext_out, out_buf, ra1, sa2, ra2, rb, sb2, rb2, acc_b,
    w_sem, rk_send, rk_recv, g_send, g_recv, nb_send, nb_recv, a1_send, a1_recv, a2_send, a2_recv, b_send, b_recv,
    rb_send, rb_recv, ra1_send, ra1_recv, ra2_send, ra2_recv, rb2_send, rb2_recv, u_send, u_recv,
):
    s, me = lax.axis_index("section"), lax.axis_index("expert")
    x, z, y = me // 16, lax.rem(me // 4, 4), lax.rem(me, 4)
    outer = jnp.logical_or(s == 0, s == 3)

    def chip(dx, dz, dy, at=None):
        ex = lax.rem(x + dx, 2) * 16 + lax.rem(z + dz + 4, 4) * 4 + lax.rem(y + dy, 4)
        return (s if at is None else at, ex)

    def send(src, dst, ssem, rsem, to):
        pltpu.make_async_remote_copy(
            src_ref=src, dst_ref=dst, send_sem=ssem, recv_sem=rsem, device_id=to, device_id_type=MESH
        ).start()

    def got(ref, sem):
        pltpu.make_async_remote_copy(
            src_ref=ref, dst_ref=ref, send_sem=sem, recv_sem=sem, device_id=chip(0, 0, 1), device_id_type=MESH
        ).wait_recv()

    def sent(ref, sem):
        pltpu.make_async_remote_copy(
            src_ref=ref, dst_ref=ref, send_sem=sem, recv_sem=sem, device_id=chip(0, 0, 1), device_id_type=MESH
        ).wait_send()

    offs = [(j % 2, (j // 2) * 2 + c) for c in range(2) for j in range(4)]

    copy_in = pltpu.make_async_copy(w_in_hbm, w_in, w_sem.at[0])
    copy_down = pltpu.make_async_copy(w_down_hbm, w_down, w_sem.at[1])
    copy_in.start()
    copy_down.start()

    barrier = pltpu.get_barrier_semaphore()
    for dx, dz in offs[1:]:
        pl.semaphore_signal(barrier, inc=1, device_id=chip(dx, dz, 0), device_id_type=MESH)
    for m in (1, 2, 3):
        pl.semaphore_signal(barrier, inc=1, device_id=chip(0, 0, m), device_id_type=MESH)
    for ds in (1, 3):
        pl.semaphore_signal(barrier, inc=1, device_id=(lax.rem(s + ds, 4), me), device_id_type=MESH)

    row, lane = iota((128, 128), 0), iota((128, 128), 1)
    o = row // 16
    dz_of = lax.rem(o // 2, 2) * 2 + o // 4
    expert_of = lax.rem(x + lax.rem(o, 2), 2) * 4 + lax.rem(z + dz_of, 4)
    onehot[...] = (lane == expert_of).astype(BF)
    r, c = iota((224, 256), 0), iota((224, 256), 1)
    sel[...] = (c == lax.rem(r, 32) * 8 + r // 32).astype(BF)
    r, c = iota((256, 224), 0), iota((256, 224), 1)
    pack[...] = (r == lax.rem(c, 32) * 8 + c // 32).astype(BF)
    lower = (iota((TOK, TOK), 0) > iota((TOK, TOK), 1)).astype(BF)
    gates[:, 0] = jnp.zeros((2, TOK, 128), BF)
    rk[0] = jnp.zeros((2, TOK, 128), BF)

    def named(step):
        direction = jnp.where(s < 2, step, 1 - step)
        pair = routes_ref[direction]
        number = iota((TOK, EXPERTS), 1)
        return jnp.logical_or(pair[:, 0:1] == number, pair[:, 1:2] == number)

    for step in range(2):
        names = named(step)
        rank = mm(lower, names.astype(F32).astype(BF))
        kept = jnp.logical_and(names, rank < caps_ref[...].astype(F32))
        rk[0, step, :, 0:EXPERTS] = jnp.where(kept, rank, LOST).astype(BF)

    @pl.when(outer)
    def _():
        u_buf[0] = batches_ref[order_ref[jnp.where(s == 0, 0, 1)]]

    pl.semaphore_wait(barrier, 12)
    for m in (1, 2, 3):
        send(rk.at[0], rk.at[4 - m], rk_send, rk_recv, chip(0, 0, m))

    def layer(step, carry):
        direction = jnp.where(s < 2, step, 1 - step)

        @pl.when(jnp.logical_not(jnp.logical_and(step == 0, outer)))
        def _():
            got(u_buf.at[step], u_recv.at[step])

        total = jnp.zeros((TOK, 512), F32)
        for i in range(D // 512):
            v = u_buf[step, :, i * 512:(i + 1) * 512].astype(F32)
            total = total + v * v
        inv = lax.rsqrt(jnp.sum(total, axis=1, keepdims=True) * (1.0 / D) + 1e-06)

        def norm_half(first):
            for i in range(first, first + HALF, 256):
                v = u_buf[step, :, i:i + 256].astype(F32)
                normed[:, i:i + 256] = (v * inv * gain_ref[:, i:i + 256]).astype(BF)

        norm_half(HALF)
        for m in (1, 2, 3):
            send(normed.at[:, HALF:D], nb.at[step, 3 - m], nb_send, nb_recv.at[step, 3 - m], chip(0, 0, m))
        norm_half(0)

        def packer(ranks):
            rt = nt(onehot[...], ranks)
            main = (rt == lax.rem(iota((128, TOK), 0), 16).astype(F32)).astype(BF)
            rt7 = nt(onehot[...], jnp.concatenate([ranks] * NBLK, axis=0))
            rw, cl = iota((128, TOK * NBLK), 0), iota((128, TOK * NBLK), 1)
            want = (16 + lax.rem(rw, 16) // 8).astype(F32)
            ext = jnp.logical_and(rt7 == want, lax.rem(rw, 8) == cl // TOK).astype(BF)
            return main, ext

        def packed(ranks, source, put):
            main, ext = packer(ranks)
            for i in range(NBLK):
                put(i * BLK, mm(main, source(i)).astype(BF))
            stack = jnp.concatenate([source(i) for i in range(NBLK)], axis=0)
            put(HALF, mm(ext, stack).astype(BF))

        def put_a(at, v):
            x_buf[step, 0, 0:16, at:at + BLK] = v[0:16]
            sa[:, :, at:at + BLK] = v[16:128].reshape(7, 16, BLK)

        packed(rk[0, step], lambda i: normed[:, i * BLK:(i + 1) * BLK], put_a)
        for i, (dx, dz) in enumerate(offs):
            if i:
                ch, j = i // 4, i % 4
                send(
                    sa.at[i - 1], x_buf.at[step, ch, j * 64:j * 64 + 16, 0:WIDE],
                    a1_send, a1_recv.at[step, i], chip(dx, dz, 0),
                )

        def second(d):
            def put_b(at, v):
                x_buf[step, 0, d * 16:d * 16 + 16, WIDE + at:WIDE + at + BLK] = v[0:16]
                sb[:, d * 16:d * 16 + 16, at:at + BLK] = v[16:128].reshape(7, 16, BLK)

            if d == 0:
                packed(rk[0, step], lambda i: normed[:, HALF + i * BLK:HALF + (i + 1) * BLK], put_b)
            else:
                packed(rk[d, step], lambda i: nb[step, d - 1, :, i * BLK:(i + 1) * BLK], put_b)
            for i, (dx, dz) in enumerate(offs):
                if i:
                    ch, j = i // 4, i % 4
                    at = j * 64 + d * 16
                    send(
                        sb.at[i - 1, d * 16:d * 16 + 16], x_buf.at[step, ch, at:at + 16, WIDE:2 * WIDE],
                        b_send, b_recv.at[step, ch], chip(dx, dz, 0),
                    )

        def forward(i):
            ch, j = i // 4, i % 4
            if i:
                got(x_buf.at[step, ch, j * 64:j * 64 + 16, 0:WIDE], a1_recv.at[step, i])
            for m in (1, 3, 2):
                at = j * 64 + (4 - m) * 16
                send(
                    x_buf.at[step, ch, j * 64:j * 64 + 16, 0:WIDE], x_buf.at[step, ch, at:at + 16, 0:WIDE],
                    a2_send, a2_recv.at[step, ch], chip(0, 0, m),
                )

        forward(0)
        second(0)
        forward(1)
        forward(2)

        @pl.when(step == 0)
        def _():
            got(rk.at[1:4], rk_recv)

        for d in (1, 3):
            got(nb.at[step, d - 1], nb_recv.at[step, d - 1])
            second(d)
            forward(d + 2)
        forward(4)
        got(nb.at[step, 1], nb_recv.at[step, 1])
        second(2)
        forward(6)
        forward(7)

        router = router_ref[...]
        high = router.astype(BF)
        low = (router - high.astype(F32)).astype(BF)
        scores = jax.nn.sigmoid(mm(normed[...], high) + mm(normed[...], low))
        chosen = jnp.sum(jnp.where(named(step), scores, 0.0), axis=1, keepdims=True)
        gates[step, 0, :, 0:EXPERTS] = (2.5 * scores / chosen).astype(BF)
        for m in (1, 2, 3):
            send(gates.at[step, 0], gates.at[step, 4 - m], g_send, g_recv.at[step], chip(0, 0, m))

        @pl.when(step == 0)
        def _():
            copy_in.wait()
            copy_down.wait()

        for ch in range(2):
            xs = x_buf.at[step, ch]
            ob = out_buf.at[ch]
            got(x_buf.at[step, ch, 0:192, 0:WIDE], a2_recv.at[step, ch])
            got(x_buf.at[step, ch, 0:192 + 64 * ch, 0:WIDE], b_recv.at[step, ch])
            for p in range(2):
                spread = mm(sel[...], xs[0:ROWS, p * WIDE + HALF:(p + 1) * WIDE]).astype(BF)
                for i in range(NBLK):
                    xs[ROWS:XROWS, p * WIDE + i * BLK:p * WIDE + (i + 1) * BLK] = spread[i * 32:(i + 1) * 32]

            def up(n, carry):
                cols = pl.ds(pl.multiple_of(n * 256, 256), 256)
                g, v = (
                    mm(xs[:, 0:HALF], w_in[q, 0:HALF, cols]) + mm(xs[:, WIDE:WIDE + HALF], w_in[q, HALF:D, cols])
                    for q in range(2)
                )
                hidden[:, cols] = (jax.nn.silu(g) * v).astype(BF)
                return carry

            lax.fori_loop(0, HID // 256, up, 0)

            for p in (1, 0):
                def down(n, carry):
                    v = mm(hidden[...], w_down[:, pl.ds(pl.multiple_of(p * HALF + n * BLK, BLK), BLK)]).astype(BF)
                    ob[0:ROWS, pl.ds(pl.multiple_of(p * WIDE + n * BLK, BLK), BLK)] = v[0:ROWS]
                    ext_out[pl.ds(pl.multiple_of(n * 32, 32), 32), :] = v[ROWS:XROWS]
                    return carry

                lax.fori_loop(0, NBLK, down, 0)
                ob[0:ROWS, p * WIDE + HALF:(p + 1) * WIDE] = mm(pack[...], ext_out[...]).astype(BF)
                for j in range(4):
                    i = ch * 4 + j
                    dx, dz = offs[i]
                    if p == 1:
                        if i == 0:
                            rb[step, 0] = ob[0:64, WIDE:2 * WIDE]
                        else:
                            send(
                                ob.at[j * 64:j * 64 + 64, WIDE:2 * WIDE], rb.at[step, i],
                                rb_send, rb_recv.at[step], chip(dx, -dz, 0),
                            )
                    else:
                        for m in (1, 3, 2):
                            send(
                                ob.at[j * 64 + m * 16:j * 64 + m * 16 + 16, 0:WIDE],
                                ra1.at[step, ch, 3 - m, j * 16:j * 16 + 16],
                                ra1_send, ra1_recv.at[step, ch], chip(0, 0, m),
                            )

        for ch in range(2):
            got(ra1.at[step, ch], ra1_recv.at[step, ch])
            for j in range(4):
                i = ch * 4 + j
                dx, dz = offs[i]
                v = out_buf[ch, j * 64:j * 64 + 16, 0:WIDE].astype(F32)
                for m in range(3):
                    v = v + ra1[step, ch, m, j * 16:j * 16 + 16].astype(F32)
                if i == 0:
                    ra2[step, 0] = v.astype(BF)
                else:
                    sa2[i - 1] = v.astype(BF)
                    send(sa2.at[i - 1], ra2.at[step, i], ra2_send, ra2_recv.at[step], chip(dx, -dz, 0))

        def weights(ranks, gate):
            rt, gt = nt(ranks, onehot[...]), nt(gate, onehot[...])
            main = jnp.where(rt == lax.rem(iota((TOK, 128), 1), 16).astype(F32), gt, 0.0).astype(BF)
            rw, cl = iota((TOK * NBLK, 128), 0), iota((TOK * NBLK, 128), 1)
            want = (16 + lax.rem(cl, 16) // 8).astype(F32)
            take = jnp.logical_and(
                jnp.concatenate([rt] * NBLK, axis=0) == want, lax.rem(cl, 8) == rw // TOK
            )
            return main, jnp.where(take, jnp.concatenate([gt] * NBLK, axis=0), 0.0).astype(BF)

        got(gates.at[step, 1:4], g_recv.at[step])
        got(rb.at[step, 1:8], rb_recv.at[step])
        for d in (2, 1, 3, 0):
            main, ext = weights(rk[d, step], gates[step, d])
            over = mm(ext, rb[step, :, d * 16:d * 16 + 16, HALF:WIDE].reshape(128, BLK))
            for i in range(NBLK):
                v = mm(main, rb[step, :, d * 16:d * 16 + 16, i * BLK:(i + 1) * BLK].reshape(128, BLK))
                v = v + over[i * TOK:(i + 1) * TOK]
                if d == 0:
                    acc_b[:, i * BLK:(i + 1) * BLK] = v
                else:
                    sb2[d - 1, :, i * BLK:(i + 1) * BLK] = v.astype(BF)
            if d:
                send(sb2.at[d - 1], rb2.at[step, 3 - d], rb2_send, rb2_recv.at[step], chip(0, 0, d))

        got(ra2.at[step, 1:8], ra2_recv.at[step])
        main, ext = weights(rk[0, step], gates[step, 0])
        over = mm(ext, ra2[step, :, :, HALF:WIDE].reshape(128, BLK))
        for i in range(NBLK):
            cols = slice(i * BLK, (i + 1) * BLK)
            v = mm(main, ra2[step, :, :, cols].reshape(128, BLK)) + over[i * TOK:(i + 1) * TOK]
            out_ref[direction, :, cols] = (u_buf[step, :, cols].astype(F32) + v).astype(BF)
        got(rb2.at[step], rb2_recv.at[step])
        for i in range(NBLK):
            cols, at = slice(i * BLK, (i + 1) * BLK), slice(HALF + i * BLK, HALF + (i + 1) * BLK)
            v = acc_b[:, cols]
            for m in range(3):
                v = v + rb2[step, m, :, cols].astype(F32)
            out_ref[direction, :, at] = (u_buf[step, :, at].astype(F32) + v).astype(BF)

        target = jnp.where(direction == 0, s + 1, s - 1)
        relays = jnp.logical_and(target >= 0, target <= 3)
        target_step = jnp.where(jnp.logical_and(step == 0, outer), 0, 1)

        @pl.when(relays)
        def _():
            send(out_ref.at[direction], u_buf.at[target_step], u_send, u_recv.at[target_step], (target, me))

        sent(nb.at[step], nb_send)
        sent(sa, a1_send)
        sent(out_buf.at[:, 0:192, 0:WIDE], a2_send)
        sent(sb, b_send)
        sent(gates.at[step, 1:4], g_send)
        sent(sb, rb_send)
        sent(out_buf.at[:, 0:192, 0:WIDE], ra1_send)
        sent(sa2, ra2_send)
        sent(sb2, rb2_send)

        @pl.when(relays)
        def _():
            sent(u_buf.at[step], u_send)

        return carry

    lax.fori_loop(0, 2, layer, 0)
    sent(rk.at[1:4], rk_send)


def local(batches, order, gains, router, routes, caps, w_in, w_down):
    vmem, hbm = pl.BlockSpec(memory_space=pltpu.VMEM), pl.BlockSpec(memory_space=pl.ANY)
    dma = pltpu.SemaphoreType.DMA
    out = pl.pallas_call(
        kernel,
        out_shape=jax.ShapeDtypeStruct((2, TOK, D), BF),
        in_specs=[pl.BlockSpec(memory_space=pltpu.SMEM), vmem, vmem, vmem, vmem, vmem, hbm, hbm],
        out_specs=vmem,
        scratch_shapes=[
            pltpu.VMEM((2, D, HID), BF),
            pltpu.VMEM((HID, D), BF),
            pltpu.VMEM((2, TOK, D), BF),
            pltpu.VMEM((TOK, D), BF),
            pltpu.VMEM((128, 128), BF),
            pltpu.VMEM((4, 2, TOK, 128), BF),
            pltpu.VMEM((2, 4, TOK, 128), BF),
            pltpu.VMEM((224, 256), BF),
            pltpu.VMEM((256, 224), BF),
            pltpu.VMEM((2, 3, TOK, HALF), BF),
            pltpu.VMEM((2, 2, XROWS, 2 * WIDE), BF),
            pltpu.VMEM((7, 16, WIDE), BF),
            pltpu.VMEM((7, 64, WIDE), BF),
            pltpu.VMEM((XROWS, HID), BF),
            pltpu.VMEM((224, 256), BF),
            pltpu.VMEM((2, ROWS, 2 * WIDE), BF),
            pltpu.VMEM((2, 2, 3, 64, WIDE), BF),
            pltpu.VMEM((7, 16, WIDE), BF),
            pltpu.VMEM((2, 8, 16, WIDE), BF),
            pltpu.VMEM((2, 8, 64, WIDE), BF),
            pltpu.VMEM((3, TOK, HALF), BF),
            pltpu.VMEM((2, 3, TOK, HALF), BF),
            pltpu.VMEM((TOK, HALF), F32),
            dma((2,)),
            dma, dma,
            dma, dma((2,)),
            dma, dma((2, 3)),
            dma, dma((2, 8)),
            dma, dma((2, 2)),
            dma, dma((2, 2)),
            dma, dma((2,)),
            dma, dma((2, 2)),
            dma, dma((2,)),
            dma, dma((2,)),
            dma, dma((2,)),
        ],
        compiler_params=pltpu.CompilerParams(
            collective_id=0, has_side_effects=True, vmem_limit_bytes=60 << 20
        ),
        name="relay",
    )(order, batches, gains, router[0], routes[0], caps, w_in[0], w_down[0])
    return out[None]


def solution(mesh):
    placed = (
        P(None, "expert", None),
        P(),
        P("section", None),
        P("section", None, None),
        P("section", None, "expert", None),
        P("section", None),
        P("section", None, None, "expert"),
        P("section", "expert", None),
    )
    return jax.shard_map(
        local,
        mesh=mesh,
        in_specs=placed,
        out_specs=P("section", None, "expert", None),
        check_vma=False,
    )
```

```python
import jax
import jax.numpy as jnp
from jax import lax
from jax.experimental import pallas as pl
from jax.experimental.pallas import tpu as pltpu
from jax.sharding import PartitionSpec as P

MESH = pl.DeviceIdType.MESH
BF, F32, I32 = jnp.bfloat16, jnp.float32, jnp.int32

D = 3584
EXPERTS = 8
HALF = D // 2
BLK = 256
NBLK = HALF // BLK
WIDE = HALF + BLK
TOK = 64
HID = 512
ROWS = 256
XROWS = 288
LOST = 99.0


def iota(shape, dim):
    return lax.broadcasted_iota(I32, shape, dim)


def nt(a, b):
    return lax.dot_general(a, b, (((1,), (1,)), ((), ())), preferred_element_type=F32)


def mm(a, b):
    return jnp.dot(a, b, preferred_element_type=F32)


def kernel(
    order_ref, batches_ref, gain_ref, router_ref, routes_ref, caps_ref, w_in_hbm, w_down_hbm, out_ref,
    w_in, w_down, u_buf, normed, onehot, rk_own, rk_near, gates_own, gates_near, sel, pack,
    nb, x_buf, sa, sb, hidden, ext_out, out_buf, part, sa2, sn2, ra2, rn2, s3, r3,
    w_sem, rk_send, rk_recv, g_send, g_recv, nb_send, nb_recv, a1_send, a1_recv, b_send, b_recv, a2_send, a2_recv,
    part_send, part_recv, ra2_send, ra2_recv, rn2_send, rn2_recv, r3_send, r3_recv, u_send, u_recv,
):
    s, me = lax.axis_index("section"), lax.axis_index("expert")
    x, z, y = me // 16, lax.rem(me // 4, 4), lax.rem(me, 4)
    outer = jnp.logical_or(s == 0, s == 3)

    def chip(dx, dz, dy):
        return (s, lax.rem(x + dx, 2) * 16 + lax.rem(z + dz + 4, 4) * 4 + lax.rem(y + dy, 4))

    def send(src, dst, ssem, rsem, to):
        pltpu.make_async_remote_copy(
            src_ref=src, dst_ref=dst, send_sem=ssem, recv_sem=rsem, device_id=to, device_id_type=MESH
        ).start()

    def got(ref, sem):
        pltpu.make_async_remote_copy(
            src_ref=ref, dst_ref=ref, send_sem=sem, recv_sem=sem, device_id=chip(0, 0, 1), device_id_type=MESH
        ).wait_recv()

    def sent(ref, sem):
        pltpu.make_async_remote_copy(
            src_ref=ref, dst_ref=ref, send_sem=sem, recv_sem=sem, device_id=chip(0, 0, 1), device_id_type=MESH
        ).wait_send()

    offs = [(j % 2, (j // 2) * 2 + c) for c in range(2) for j in range(4)]
    toward, near = (1, 3), (3, 1)

    def lanes(p):
        return slice(p * WIDE, (p + 1) * WIDE)

    copy_in = pltpu.make_async_copy(w_in_hbm, w_in, w_sem.at[0])
    copy_down = pltpu.make_async_copy(w_down_hbm, w_down, w_sem.at[1])
    copy_in.start()
    copy_down.start()

    barrier = pltpu.get_barrier_semaphore()
    for dx, dz in offs[1:]:
        pl.semaphore_signal(barrier, inc=1, device_id=chip(dx, dz, 0), device_id_type=MESH)
    for m in (1, 3):
        pl.semaphore_signal(barrier, inc=1, device_id=chip(0, 0, m), device_id_type=MESH)
    for ds in (1, 3):
        pl.semaphore_signal(barrier, inc=1, device_id=(lax.rem(s + ds, 4), me), device_id_type=MESH)

    row, lane = iota((128, 128), 0), iota((128, 128), 1)
    o = row // 16
    dz_of = lax.rem(o // 2, 2) * 2 + o // 4
    expert_of = lax.rem(x + lax.rem(o, 2), 2) * 4 + lax.rem(z + dz_of, 4)
    onehot[...] = (lane == expert_of).astype(BF)
    r, c = iota((224, 256), 0), iota((224, 256), 1)
    sel[...] = (c == lax.rem(r, 32) * 8 + r // 32).astype(BF)
    r, c = iota((256, 224), 0), iota((256, 224), 1)
    pack[...] = (r == lax.rem(c, 32) * 8 + c // 32).astype(BF)
    lower = (iota((TOK, TOK), 0) > iota((TOK, TOK), 1)).astype(BF)
    eye = (iota((TOK, TOK), 0) == iota((TOK, TOK), 1)).astype(BF)
    gates_own[...] = jnp.zeros_like(gates_own)
    rk_own[...] = jnp.zeros_like(rk_own)

    def named(step):
        direction = jnp.where(s < 2, step, 1 - step)
        pair = routes_ref[direction]
        number = iota((EXPERTS, TOK), 0)
        names = jnp.logical_or(pair[0:1] == number, pair[1:2] == number)
        return names.astype(F32).astype(BF)

    for step in range(2):
        names = named(step)
        rank = nt(lower, names)
        kept = jnp.logical_and(nt(eye, names) > 0.5, rank < caps_ref[...].astype(F32))
        rk_own[step, :, 0:EXPERTS] = jnp.where(kept, rank, LOST).astype(BF)

    @pl.when(outer)
    def _():
        u_buf[0] = batches_ref[order_ref[jnp.where(s == 0, 0, 1)]]

    pl.semaphore_wait(barrier, 11)
    for p in range(2):
        send(rk_own, rk_near.at[p], rk_send, rk_recv, chip(0, 0, toward[p]))

    def layer(step, carry):
        direction = jnp.where(s < 2, step, 1 - step)

        @pl.when(jnp.logical_not(jnp.logical_and(step == 0, outer)))
        def _():
            got(u_buf.at[step], u_recv.at[step])

        total = jnp.zeros((TOK, 512), F32)
        for i in range(D // 512):
            v = u_buf[step, :, i * 512:(i + 1) * 512].astype(F32)
            total = total + v * v
        inv = lax.rsqrt(jnp.sum(total, axis=1, keepdims=True) * (1.0 / D) + 1e-06)
        for p in range(2):
            for i in range(p * HALF, (p + 1) * HALF, 256):
                v = u_buf[step, :, i:i + 256].astype(F32)
                normed[:, i:i + 256] = (v * inv * gain_ref[:, i:i + 256]).astype(BF)
            send(
                normed.at[:, p * HALF:(p + 1) * HALF], nb.at[step, p],
                nb_send, nb_recv.at[step, p], chip(0, 0, toward[p]),
            )

        def packer(ranks):
            rt = nt(onehot[...], ranks)
            main = (rt == lax.rem(iota((128, TOK), 0), 16).astype(F32)).astype(BF)
            rt7 = nt(onehot[...], jnp.concatenate([ranks] * NBLK, axis=0))
            rw, cl = iota((128, TOK * NBLK), 0), iota((128, TOK * NBLK), 1)
            want = (16 + lax.rem(rw, 16) // 8).astype(F32)
            ext = jnp.logical_and(rt7 == want, lax.rem(rw, 8) == cl // TOK).astype(BF)
            return main, ext

        def packed(tables, source, put):
            main, ext = tables
            for i in range(NBLK):
                put(i * BLK, mm(main, source(i)).astype(BF))
            stack = jnp.concatenate([source(i) for i in range(NBLK)], axis=0)
            put(HALF, mm(ext, stack).astype(BF))

        def send_own(i):
            (dx, dz), ch, j = offs[i], i // 4, i % 4
            send(sa.at[i - 1], x_buf.at[step, ch, j * 16:j * 16 + 16], a1_send, a1_recv.at[step, i], chip(dx, dz, 0))

        def send_near(p, i):
            (dx, dz), ch, at = offs[i], i // 4, near[p] * 64 + i % 4 * 16
            send(
                sb.at[p, i - 1], x_buf.at[step, ch, at:at + 16, lanes(p)],
                b_send, b_recv.at[step, p * 8 + i], chip(dx, dz, 0),
            )

        def forward_own(i):
            ch, j = i // 4, i % 4
            if i:
                got(x_buf.at[step, ch, j * 16:j * 16 + 16], a1_recv.at[step, i])
            for p in range(2):
                at = toward[p] * 64 + j * 16
                send(
                    x_buf.at[step, ch, j * 16:j * 16 + 16, lanes(p)], x_buf.at[step, ch, at:at + 16, lanes(p)],
                    a2_send, a2_recv.at[step, ch], chip(0, 0, near[p]),
                )

        def forward_near(p, i):
            ch, j = i // 4, i % 4
            at, to = near[p] * 64 + j * 16, 128 + j * 16
            if i:
                got(x_buf.at[step, ch, at:at + 16, lanes(p)], b_recv.at[step, p * 8 + i])
            send(
                x_buf.at[step, ch, at:at + 16, lanes(p)], x_buf.at[step, ch, to:to + 16, lanes(p)],
                a2_send, a2_recv.at[step, ch], chip(0, 0, toward[p]),
            )

        tables = packer(rk_own[step])
        for p in range(2):
            def put_own(at, v):
                x_buf[step, 0, 0:16, p * WIDE + at:p * WIDE + at + BLK] = v[0:16]
                sa[:, :, p * WIDE + at:p * WIDE + at + BLK] = v[16:128].reshape(7, 16, BLK)

            packed(tables, lambda i: normed[:, p * HALF + i * BLK:p * HALF + (i + 1) * BLK], put_own)
        for i in (1, 2, 3):
            send_own(i)
        forward_own(0)

        @pl.when(step == 0)
        def _():
            got(rk_near, rk_recv)

        for p in range(2):
            def put_near(at, v):
                first = near[p] * 64
                x_buf[step, 0, first:first + 16, p * WIDE + at:p * WIDE + at + BLK] = v[0:16]
                sb[p, :, :, at:at + BLK] = v[16:128].reshape(7, 16, BLK)

            tables = packer(rk_near[p, step])
            got(nb.at[step, p], nb_recv.at[step, p])
            packed(tables, lambda i: nb[step, p, :, i * BLK:(i + 1) * BLK], put_near)
            for i in (1, 2, 3):
                send_near(p, i)
            forward_near(p, 0)
        for i in (1, 2, 3):
            forward_own(i)
        for i in range(4, 8):
            send_own(i)
        for p in range(2):
            for i in (1, 2, 3):
                forward_near(p, i)
        for i in range(4, 8):
            for p in range(2):
                send_near(p, i)

        router = router_ref[...]
        high = router.astype(BF)
        low = (router - high.astype(F32)).astype(BF)
        scores = jax.nn.sigmoid(nt(normed[...], high) + nt(normed[...], low))
        chosen = jnp.sum(nt(eye, named(step)) * scores, axis=1, keepdims=True)
        gates_own[step, :, 0:EXPERTS] = (2.5 * scores / chosen).astype(BF)
        for p in range(2):
            send(gates_own.at[step], gates_near.at[step, p], g_send, g_recv.at[step], chip(0, 0, toward[p]))

        for i in range(4, 8):
            forward_own(i)

        @pl.when(step == 0)
        def _():
            copy_in.wait()
            copy_down.wait()

        def arrived(ch):
            got(x_buf.at[step, ch, 0:ROWS, 0:WIDE], a2_recv.at[step, ch])
            for p in range(2):
                spread = mm(sel[...], x_buf[step, ch, 0:ROWS, p * WIDE + HALF:(p + 1) * WIDE]).astype(BF)
                for i in range(NBLK):
                    cols = slice(p * WIDE + i * BLK, p * WIDE + (i + 1) * BLK)
                    x_buf[step, ch, ROWS:XROWS, cols] = spread[i * 32:(i + 1) * 32]

        def up(ch, n):
            cols = slice(n * 256, (n + 1) * 256)
            g, v = (
                mm(x_buf[step, ch, :, 0:HALF], w_in[q, 0:HALF, cols])
                + mm(x_buf[step, ch, :, WIDE:WIDE + HALF], w_in[q, HALF:D, cols])
                for q in range(2)
            )
            hidden[:, cols] = (jax.nn.silu(g) * v).astype(BF)

        def down(ch, p):
            def tile(n, carry):
                v = mm(hidden[...], w_down[:, pl.ds(pl.multiple_of(p * HALF + n * BLK, BLK), BLK)]).astype(BF)
                out_buf[ch, 0:ROWS, pl.ds(pl.multiple_of(p * WIDE + n * BLK, BLK), BLK)] = v[0:ROWS]
                ext_out[pl.ds(pl.multiple_of(n * 32, 32), 32), :] = v[ROWS:XROWS]
                return carry

            lax.fori_loop(0, NBLK, tile, 0)
            out_buf[ch, 0:ROWS, p * WIDE + HALF:(p + 1) * WIDE] = mm(pack[...], ext_out[...]).astype(BF)

        def send_part(ch, p, q):
            first, to = (128, near[p]) if q else (toward[p] * 64, toward[p])
            send(
                out_buf.at[ch, first:first + 64, lanes(p)], part.at[step, ch, p * 2 + q],
                part_send, part_recv.at[step, ch * 4 + p * 2 + q], chip(0, 0, to),
            )

        def back(ch, p, q):
            got(part.at[step, ch, p * 2 + q], part_recv.at[step, ch * 4 + p * 2 + q])
            for j in range(4):
                i = ch * 4 + j
                dx, dz = offs[i]
                first = near[p] * 64 * q + j * 16
                v = out_buf[ch, first:first + 16, lanes(p)].astype(F32)
                v = (v + part[step, ch, p * 2 + q, j * 16:j * 16 + 16].astype(F32)).astype(BF)
                if q and i:
                    sn2[p, i - 1] = v
                    send(sn2.at[p, i - 1], rn2.at[step, p, i], rn2_send, rn2_recv.at[step, p], chip(dx, -dz, 0))
                elif q:
                    rn2[step, p, 0] = v
                elif i:
                    sa2[i - 1, :, lanes(p)] = v
                    if p:
                        send(sa2.at[i - 1], ra2.at[step, i], ra2_send, ra2_recv.at[step], chip(dx, -dz, 0))
                else:
                    ra2[step, 0, :, lanes(p)] = v

        arrived(0)
        up(0, 0)
        for p in range(2):
            for i in range(4, 8):
                forward_near(p, i)
        up(0, 1)
        for p in range(2):
            down(0, p)
            send_part(0, p, 1)
            send_part(0, p, 0)
        arrived(1)
        up(1, 0)
        up(1, 1)
        back(0, 0, 1)
        down(1, 0)
        send_part(1, 0, 1)
        back(0, 1, 1)
        down(1, 1)
        send_part(1, 1, 1)
        send_part(1, 0, 0)
        send_part(1, 1, 0)
        back(0, 0, 0)
        back(0, 1, 0)
        for q in (1, 0):
            for p in range(2):
                back(1, p, q)

        def weights(ranks, gate):
            rt, gt = nt(ranks, onehot[...]), nt(gate, onehot[...])
            main = jnp.where(rt == lax.rem(iota((TOK, 128), 1), 16).astype(F32), gt, 0.0).astype(BF)
            rw, cl = iota((TOK * NBLK, 128), 0), iota((TOK * NBLK, 128), 1)
            want = (16 + lax.rem(cl, 16) // 8).astype(F32)
            take = jnp.logical_and(
                jnp.concatenate([rt] * NBLK, axis=0) == want, lax.rem(cl, 8) == rw // TOK
            )
            return main, jnp.where(take, jnp.concatenate([gt] * NBLK, axis=0), 0.0).astype(BF)

        def weighed(tables, source, put):
            main, ext = tables
            over = mm(ext, source(HALF))
            for i in range(NBLK):
                put(i * BLK, mm(main, source(i * BLK)) + over[i * TOK:(i + 1) * TOK])

        got(gates_near.at[step], g_recv.at[step])
        for p in range(2):
            def put_back(at, v):
                s3[p, :, at:at + BLK] = v.astype(BF)

            tables = weights(rk_near[p, step], gates_near[step, p])
            got(rn2.at[step, p, 1:8], rn2_recv.at[step, p])
            weighed(tables, lambda at: rn2[step, p, :, :, at:at + BLK].reshape(128, BLK), put_back)
            send(s3.at[p], r3.at[step, p], r3_send, r3_recv.at[step, p], chip(0, 0, near[p]))

        tables = weights(rk_own[step], gates_own[step])
        got(ra2.at[step, 1:8], ra2_recv.at[step])
        for p in range(2):
            got(r3.at[step, p], r3_recv.at[step, p])

            def put_out(at, v):
                cols = slice(p * HALF + at, p * HALF + at + BLK)
                v = v + r3[step, p, :, at:at + BLK].astype(F32)
                out_ref[direction, :, cols] = (u_buf[step, :, cols].astype(F32) + v).astype(BF)

            weighed(tables, lambda at: ra2[step, :, :, p * WIDE + at:p * WIDE + at + BLK].reshape(128, BLK), put_out)

        target = jnp.where(direction == 0, s + 1, s - 1)
        relays = jnp.logical_and(target >= 0, target <= 3)
        target_step = jnp.where(jnp.logical_and(step == 0, outer), 0, 1)

        @pl.when(relays)
        def _():
            send(out_ref.at[direction], u_buf.at[target_step], u_send, u_recv.at[target_step], (target, me))

        sent(nb.at[step], nb_send)
        sent(sa, a1_send)
        sent(sb, b_send)
        sent(x_buf.at[step, :, 0:ROWS, 0:WIDE], a2_send)
        sent(gates_near.at[step], g_send)
        sent(part.at[step], part_send)
        sent(sa2, ra2_send)
        sent(sn2, rn2_send)
        sent(s3, r3_send)

        @pl.when(relays)
        def _():
            sent(u_buf.at[step], u_send)

        return carry

    lax.fori_loop(0, 2, layer, 0)
    sent(rk_near, rk_send)


def local(batches, order, gains, router, routes, caps, w_in, w_down):
    vmem, hbm = pl.BlockSpec(memory_space=pltpu.VMEM), pl.BlockSpec(memory_space=pl.ANY)
    dma = pltpu.SemaphoreType.DMA
    out = pl.pallas_call(
        kernel,
        out_shape=jax.ShapeDtypeStruct((2, TOK, D), BF),
        in_specs=[pl.BlockSpec(memory_space=pltpu.SMEM), vmem, vmem, vmem, vmem, vmem, hbm, hbm],
        out_specs=vmem,
        scratch_shapes=[
            pltpu.VMEM((2, D, HID), BF),
            pltpu.VMEM((HID, D), BF),
            pltpu.VMEM((2, TOK, D), BF),
            pltpu.VMEM((TOK, D), BF),
            pltpu.VMEM((128, 128), BF),
            pltpu.VMEM((2, TOK, 128), BF),
            pltpu.VMEM((2, 2, TOK, 128), BF),
            pltpu.VMEM((2, TOK, 128), BF),
            pltpu.VMEM((2, 2, TOK, 128), BF),
            pltpu.VMEM((224, 256), BF),
            pltpu.VMEM((256, 224), BF),
            pltpu.VMEM((2, 2, TOK, HALF), BF),
            pltpu.VMEM((2, 2, XROWS, 2 * WIDE), BF),
            pltpu.VMEM((7, 16, 2 * WIDE), BF),
            pltpu.VMEM((2, 7, 16, WIDE), BF),
            pltpu.VMEM((XROWS, HID), BF),
            pltpu.VMEM((224, 256), BF),
            pltpu.VMEM((2, ROWS, 2 * WIDE), BF),
            pltpu.VMEM((2, 2, 4, 64, WIDE), BF),
            pltpu.VMEM((7, 16, 2 * WIDE), BF),
            pltpu.VMEM((2, 7, 16, WIDE), BF),
            pltpu.VMEM((2, 8, 16, 2 * WIDE), BF),
            pltpu.VMEM((2, 2, 8, 16, WIDE), BF),
            pltpu.VMEM((2, TOK, HALF), BF),
            pltpu.VMEM((2, 2, TOK, HALF), BF),
            dma((2,)),
            dma, dma,
            dma, dma((2,)),
            dma, dma((2, 2)),
            dma, dma((2, 8)),
            dma, dma((2, 16)),
            dma, dma((2, 2)),
            dma, dma((2, 8)),
            dma, dma((2,)),
            dma, dma((2, 2)),
            dma, dma((2, 2)),
            dma, dma((2,)),
        ],
        compiler_params=pltpu.CompilerParams(
            collective_id=0, has_side_effects=True, vmem_limit_bytes=60 << 20
        ),
        name="relay",
    )(order, batches, gains, router[0].T, jnp.swapaxes(routes[0], 1, 2), caps, w_in[0], w_down[0])
    return out[None]


def solution(mesh):
    placed = (
        P(None, "expert", None),
        P(),
        P("section", None),
        P("section", None, None),
        P("section", None, "expert", None),
        P("section", None),
        P("section", None, None, "expert"),
        P("section", "expert", None),
    )
    return jax.shard_map(
        local,
        mesh=mesh,
        in_specs=placed,
        out_specs=P("section", None, "expert", None),
        check_vma=False,
    )
```

```python
import jax
import jax.numpy as jnp
from jax import lax
from jax.experimental import pallas as pl
from jax.experimental.pallas import tpu as pltpu
from jax.sharding import PartitionSpec as P

MESH = pl.DeviceIdType.MESH
BF, F32, I32 = jnp.bfloat16, jnp.float32, jnp.int32

D = 3584
EXPERTS = 8
HALF = D // 2
BLK = 256
NBLK = HALF // BLK
WIDE = HALF + BLK
TOK = 64
HID = 512
ROWS = 256
XROWS = 288
LOST = 99.0


def iota(shape, dim):
    return lax.broadcasted_iota(I32, shape, dim)


def nt(a, b):
    return lax.dot_general(a, b, (((1,), (1,)), ((), ())), preferred_element_type=F32)


def mm(a, b):
    return jnp.dot(a, b, preferred_element_type=F32)


def kernel(
    order_ref, batches_ref, gain_ref, router_ref, routes_ref, caps_ref, w_in_hbm, w_down_hbm, out_ref,
    w_in, w_down, u_buf, normed, onehot, rk_own, rk_near, gates_own, gates_near, pick_main, pick_ext, sel, pack,
    nb, x_buf, sa, sb, hidden, ext_out, out_buf, part, sa2, sn2, ra2, rn2, s3, r3, total_out,
    w_sem, rk_send, rk_recv, g_send, g_recv, nb_send, nb_recv, a1_send, a1_recv, b_send, b_recv, a2_send, a2_recv,
    part_send, part_recv, ra2_send, ra2_recv, rn2_send, rn2_recv, r3_send, r3_recv, u_send, u_recv,
):
    s, me = lax.axis_index("section"), lax.axis_index("expert")
    x, z, y = me // 16, lax.rem(me // 4, 4), lax.rem(me, 4)
    outer = jnp.logical_or(s == 0, s == 3)

    def chip(dx, dz, dy):
        return (s, lax.rem(x + dx, 2) * 16 + lax.rem(z + dz + 4, 4) * 4 + lax.rem(y + dy, 4))

    def send(src, dst, ssem, rsem, to):
        pltpu.make_async_remote_copy(
            src_ref=src, dst_ref=dst, send_sem=ssem, recv_sem=rsem, device_id=to, device_id_type=MESH
        ).start()

    def got(ref, sem):
        pltpu.make_async_remote_copy(
            src_ref=ref, dst_ref=ref, send_sem=sem, recv_sem=sem, device_id=chip(0, 0, 1), device_id_type=MESH
        ).wait_recv()

    def sent(ref, sem):
        pltpu.make_async_remote_copy(
            src_ref=ref, dst_ref=ref, send_sem=sem, recv_sem=sem, device_id=chip(0, 0, 1), device_id_type=MESH
        ).wait_send()

    offs = [(j % 2, (j // 2) * 2 + c) for c in range(2) for j in range(4)]
    toward, near = (1, 3), (3, 1)

    def lanes(p):
        return slice(p * WIDE, (p + 1) * WIDE)

    copy_in = pltpu.make_async_copy(w_in_hbm, w_in, w_sem.at[0])
    copy_down = pltpu.make_async_copy(w_down_hbm, w_down, w_sem.at[1])
    copy_in.start()
    copy_down.start()

    barrier = pltpu.get_barrier_semaphore()
    for dx, dz in offs[1:]:
        pl.semaphore_signal(barrier, inc=1, device_id=chip(dx, dz, 0), device_id_type=MESH)
    for m in (1, 3):
        pl.semaphore_signal(barrier, inc=1, device_id=chip(0, 0, m), device_id_type=MESH)
    for ds in (1, 3):
        pl.semaphore_signal(barrier, inc=1, device_id=(lax.rem(s + ds, 4), me), device_id_type=MESH)

    row, lane = iota((128, 128), 0), iota((128, 128), 1)
    o = row // 16
    dz_of = lax.rem(o // 2, 2) * 2 + o // 4
    expert_of = lax.rem(x + lax.rem(o, 2), 2) * 4 + lax.rem(z + dz_of, 4)
    onehot[...] = (lane == expert_of).astype(BF)
    r, c = iota((224, 256), 0), iota((224, 256), 1)
    sel[...] = (c == lax.rem(r, 32) * 8 + r // 32).astype(BF)
    r, c = iota((256, 224), 0), iota((256, 224), 1)
    pack[...] = (r == lax.rem(c, 32) * 8 + c // 32).astype(BF)
    lower = (iota((TOK, TOK), 0) > iota((TOK, TOK), 1)).astype(BF)
    eye = (iota((TOK, TOK), 0) == iota((TOK, TOK), 1)).astype(BF)
    gates_own[...] = jnp.zeros_like(gates_own)
    rk_own[...] = jnp.zeros_like(rk_own)

    def named(step):
        direction = jnp.where(s < 2, step, 1 - step)
        pair = routes_ref[direction]
        number = iota((EXPERTS, TOK), 0)
        names = jnp.logical_or(pair[0:1] == number, pair[1:2] == number)
        return names.astype(F32).astype(BF)

    for step in range(2):
        names = named(step)
        rank = nt(lower, names)
        kept = jnp.logical_and(nt(eye, names) > 0.5, rank < caps_ref[...].astype(F32))
        rk_own[step, :, 0:EXPERTS] = jnp.where(kept, rank, LOST).astype(BF)

    @pl.when(outer)
    def _():
        u_buf[0] = batches_ref[order_ref[jnp.where(s == 0, 0, 1)]]

    pl.semaphore_wait(barrier, 11)
    for p in range(2):
        send(rk_own, rk_near.at[p], rk_send, rk_recv, chip(0, 0, toward[p]))

    def layer(step, carry):
        direction = jnp.where(s < 2, step, 1 - step)

        def packer(ranks):
            rt = nt(onehot[...], ranks)
            main = (rt == lax.rem(iota((128, TOK), 0), 16).astype(F32)).astype(BF)
            rt7 = nt(onehot[...], jnp.concatenate([ranks] * NBLK, axis=0))
            rw, cl = iota((128, TOK * NBLK), 0), iota((128, TOK * NBLK), 1)
            want = (16 + lax.rem(rw, 16) // 8).astype(F32)
            ext = jnp.logical_and(rt7 == want, lax.rem(rw, 8) == cl // TOK).astype(BF)
            return main, ext

        pick_main[0], pick_ext[0] = packer(rk_own[step])

        @pl.when(step == 0)
        def _():
            got(rk_near, rk_recv)

        for p in range(2):
            pick_main[p + 1], pick_ext[p + 1] = packer(rk_near[p, step])

        @pl.when(jnp.logical_not(jnp.logical_and(step == 0, outer)))
        def _():
            got(u_buf.at[step], u_recv.at[step])

        total = jnp.zeros((TOK, 512), F32)
        for i in range(D // 512):
            v = u_buf[step, :, i * 512:(i + 1) * 512].astype(F32)
            total = total + v * v
        inv = lax.rsqrt(jnp.sum(total, axis=1, keepdims=True) * (1.0 / D) + 1e-06)
        for p in range(2):
            for i in range(p * HALF, (p + 1) * HALF, 256):
                v = u_buf[step, :, i:i + 256].astype(F32)
                normed[:, i:i + 256] = (v * inv * gain_ref[:, i:i + 256]).astype(BF)
            send(
                normed.at[:, p * HALF:(p + 1) * HALF], nb.at[step, p],
                nb_send, nb_recv.at[step, p], chip(0, 0, toward[p]),
            )

        def packed(which, source, put):
            main, ext = pick_main[which], pick_ext[which]
            for i in range(NBLK):
                put(i * BLK, mm(main, source(i)).astype(BF))
            stack = jnp.concatenate([source(i) for i in range(NBLK)], axis=0)
            put(HALF, mm(ext, stack).astype(BF))

        def send_own(i):
            (dx, dz), ch, j = offs[i], i // 4, i % 4
            send(sa.at[i - 1], x_buf.at[step, ch, j * 16:j * 16 + 16], a1_send, a1_recv.at[step, i], chip(dx, dz, 0))

        def send_near(p, i):
            (dx, dz), ch, at = offs[i], i // 4, near[p] * 64 + i % 4 * 16
            send(
                sb.at[p, i - 1], x_buf.at[step, ch, at:at + 16, lanes(p)],
                b_send, b_recv.at[step, p * 8 + i], chip(dx, dz, 0),
            )

        def forward_own(i):
            ch, j = i // 4, i % 4
            if i:
                got(x_buf.at[step, ch, j * 16:j * 16 + 16], a1_recv.at[step, i])
            for p in range(2):
                at = toward[p] * 64 + j * 16
                send(
                    x_buf.at[step, ch, j * 16:j * 16 + 16, lanes(p)], x_buf.at[step, ch, at:at + 16, lanes(p)],
                    a2_send, a2_recv.at[step, ch], chip(0, 0, near[p]),
                )

        def forward_near(p, i):
            ch, j = i // 4, i % 4
            at, to = near[p] * 64 + j * 16, 128 + j * 16
            if i:
                got(x_buf.at[step, ch, at:at + 16, lanes(p)], b_recv.at[step, p * 8 + i])
            send(
                x_buf.at[step, ch, at:at + 16, lanes(p)], x_buf.at[step, ch, to:to + 16, lanes(p)],
                a2_send, a2_recv.at[step, ch], chip(0, 0, toward[p]),
            )

        for p in range(2):
            def put_own(at, v):
                x_buf[step, 0, 0:16, p * WIDE + at:p * WIDE + at + BLK] = v[0:16]
                sa[:, :, p * WIDE + at:p * WIDE + at + BLK] = v[16:128].reshape(7, 16, BLK)

            packed(0, lambda i: normed[:, p * HALF + i * BLK:p * HALF + (i + 1) * BLK], put_own)
        for i in range(1, 8):
            send_own(i)
        forward_own(0)

        for p in range(2):
            def put_near(at, v):
                first = near[p] * 64
                x_buf[step, 0, first:first + 16, p * WIDE + at:p * WIDE + at + BLK] = v[0:16]
                sb[p, :, :, at:at + BLK] = v[16:128].reshape(7, 16, BLK)

            got(nb.at[step, p], nb_recv.at[step, p])
            packed(p + 1, lambda i: nb[step, p, :, i * BLK:(i + 1) * BLK], put_near)
            for i in (1, 2, 3):
                send_near(p, i)
            forward_near(p, 0)
        for i in range(4, 8):
            for p in range(2):
                send_near(p, i)
        for i in range(1, 8):
            forward_own(i)

        router = router_ref[...]
        high = router.astype(BF)
        low = (router - high.astype(F32)).astype(BF)
        scores = jax.nn.sigmoid(nt(normed[...], high) + nt(normed[...], low))
        chosen = jnp.sum(nt(eye, named(step)) * scores, axis=1, keepdims=True)
        gates_own[step, :, 0:EXPERTS] = (2.5 * scores / chosen).astype(BF)
        for p in range(2):
            send(gates_own.at[step], gates_near.at[step, p], g_send, g_recv.at[step], chip(0, 0, toward[p]))

        for group in ((1, 2, 3), (4, 5, 6, 7)):
            for p in range(2):
                for i in group:
                    forward_near(p, i)

        @pl.when(step == 0)
        def _():
            copy_in.wait()
            copy_down.wait()

        def arrived(ch):
            got(x_buf.at[step, ch, 0:ROWS, 0:WIDE], a2_recv.at[step, ch])
            for p in range(2):
                spread = mm(sel[...], x_buf[step, ch, 0:ROWS, p * WIDE + HALF:(p + 1) * WIDE]).astype(BF)
                for i in range(NBLK):
                    cols = slice(p * WIDE + i * BLK, p * WIDE + (i + 1) * BLK)
                    x_buf[step, ch, ROWS:XROWS, cols] = spread[i * 32:(i + 1) * 32]

        def up(ch, n):
            cols = slice(n * 256, (n + 1) * 256)
            g, v = (
                mm(x_buf[step, ch, :, 0:HALF], w_in[q, 0:HALF, cols])
                + mm(x_buf[step, ch, :, WIDE:WIDE + HALF], w_in[q, HALF:D, cols])
                for q in range(2)
            )
            hidden[:, cols] = (jax.nn.silu(g) * v).astype(BF)

        def down(ch, p):
            for n in range(NBLK):
                v = mm(hidden[...], w_down[:, p * HALF + n * BLK:p * HALF + (n + 1) * BLK]).astype(BF)
                out_buf[ch, 0:ROWS, p * WIDE + n * BLK:p * WIDE + (n + 1) * BLK] = v[0:ROWS]
                ext_out[n * 32:(n + 1) * 32, :] = v[ROWS:XROWS]
            out_buf[ch, 0:ROWS, p * WIDE + HALF:(p + 1) * WIDE] = mm(pack[...], ext_out[...]).astype(BF)

        def send_part(ch, p, q):
            first, to = (128, near[p]) if q else (toward[p] * 64, toward[p])
            send(
                out_buf.at[ch, first:first + 64, lanes(p)], part.at[step, ch, p * 2 + q],
                part_send, part_recv.at[step, ch * 4 + p * 2 + q], chip(0, 0, to),
            )

        def back(ch, p, q):
            got(part.at[step, ch, p * 2 + q], part_recv.at[step, ch * 4 + p * 2 + q])
            for j in range(4):
                i = ch * 4 + j
                dx, dz = offs[i]
                first = near[p] * 64 * q + j * 16
                v = out_buf[ch, first:first + 16, lanes(p)].astype(F32)
                v = (v + part[step, ch, p * 2 + q, j * 16:j * 16 + 16].astype(F32)).astype(BF)
                if q and i:
                    sn2[p, i - 1] = v
                    send(sn2.at[p, i - 1], rn2.at[step, p, i], rn2_send, rn2_recv.at[step, p], chip(dx, -dz, 0))
                elif q:
                    rn2[step, p, 0] = v
                elif i:
                    sa2[i - 1, :, lanes(p)] = v
                    send(
                        sa2.at[i - 1, :, lanes(p)], ra2.at[step, i, :, lanes(p)],
                        ra2_send, ra2_recv.at[step, p], chip(dx, -dz, 0),
                    )
                else:
                    ra2[step, 0, :, lanes(p)] = v

        arrived(0)
        up(0, 0)
        up(0, 1)
        for p in range(2):
            down(0, p)
            send_part(0, p, 1)
            send_part(0, p, 0)
        arrived(1)
        up(1, 0)
        up(1, 1)
        back(0, 0, 1)
        down(1, 0)
        send_part(1, 0, 1)
        back(0, 1, 1)
        down(1, 1)
        send_part(1, 1, 1)
        send_part(1, 0, 0)
        send_part(1, 1, 0)
        back(0, 0, 0)
        back(0, 1, 0)
        for q in (1, 0):
            for p in range(2):
                back(1, p, q)

        def weights(ranks, gate):
            rt, gt = nt(ranks, onehot[...]), nt(gate, onehot[...])
            main = jnp.where(rt == lax.rem(iota((TOK, 128), 1), 16).astype(F32), gt, 0.0).astype(BF)
            rw, cl = iota((TOK * NBLK, 128), 0), iota((TOK * NBLK, 128), 1)
            want = (16 + lax.rem(cl, 16) // 8).astype(F32)
            take = jnp.logical_and(
                jnp.concatenate([rt] * NBLK, axis=0) == want, lax.rem(cl, 8) == rw // TOK
            )
            return main, jnp.where(take, jnp.concatenate([gt] * NBLK, axis=0), 0.0).astype(BF)

        def weighed(tables, source, put):
            main, ext = tables
            over = mm(ext, source(HALF))
            for i in range(NBLK):
                put(i * BLK, mm(main, source(i * BLK)) + over[i * TOK:(i + 1) * TOK])

        got(gates_near.at[step], g_recv.at[step])
        for p in range(2):
            def put_back(at, v):
                s3[p, :, at:at + BLK] = v.astype(BF)

            tables = weights(rk_near[p, step], gates_near[step, p])
            got(rn2.at[step, p, 1:8], rn2_recv.at[step, p])
            weighed(tables, lambda at: rn2[step, p, :, :, at:at + BLK].reshape(128, BLK), put_back)
            send(s3.at[p], r3.at[step, p], r3_send, r3_recv.at[step, p], chip(0, 0, near[p]))

        tables = weights(rk_own[step], gates_own[step])
        for p in range(2):
            got(ra2.at[step, 1:8, :, lanes(p)], ra2_recv.at[step, p])

            def put_sum(at, v):
                cols = slice(p * HALF + at, p * HALF + at + BLK)
                total_out[:, cols] = u_buf[step, :, cols].astype(F32) + v

            weighed(tables, lambda at: ra2[step, :, :, p * WIDE + at:p * WIDE + at + BLK].reshape(128, BLK), put_sum)

        target = jnp.where(direction == 0, s + 1, s - 1)
        relays = jnp.logical_and(target >= 0, target <= 3)
        target_step = jnp.where(jnp.logical_and(step == 0, outer), 0, 1)
        for p in range(2):
            got(r3.at[step, p], r3_recv.at[step, p])
            half = slice(p * HALF, (p + 1) * HALF)
            for i in range(NBLK):
                cols = slice(p * HALF + i * BLK, p * HALF + (i + 1) * BLK)
                v = total_out[:, cols] + r3[step, p, :, i * BLK:(i + 1) * BLK].astype(F32)
                out_ref[direction, :, cols] = v.astype(BF)

            @pl.when(relays)
            def _():
                send(
                    out_ref.at[direction, :, half], u_buf.at[target_step, :, half],
                    u_send, u_recv.at[target_step], (target, me),
                )

        sent(nb.at[step], nb_send)
        sent(sa, a1_send)
        sent(sb, b_send)
        sent(x_buf.at[step, :, 0:ROWS, 0:WIDE], a2_send)
        sent(gates_near.at[step], g_send)
        sent(part.at[step], part_send)
        sent(sa2, ra2_send)
        sent(sn2, rn2_send)
        sent(s3, r3_send)

        @pl.when(relays)
        def _():
            sent(u_buf.at[step], u_send)

        return carry

    lax.fori_loop(0, 2, layer, 0)
    sent(rk_near, rk_send)


def local(batches, order, gains, router, routes, caps, w_in, w_down):
    vmem, hbm = pl.BlockSpec(memory_space=pltpu.VMEM), pl.BlockSpec(memory_space=pl.ANY)
    dma = pltpu.SemaphoreType.DMA
    out = pl.pallas_call(
        kernel,
        out_shape=jax.ShapeDtypeStruct((2, TOK, D), BF),
        in_specs=[pl.BlockSpec(memory_space=pltpu.SMEM), vmem, vmem, vmem, vmem, vmem, hbm, hbm],
        out_specs=vmem,
        scratch_shapes=[
            pltpu.VMEM((2, D, HID), BF),
            pltpu.VMEM((HID, D), BF),
            pltpu.VMEM((2, TOK, D), BF),
            pltpu.VMEM((TOK, D), BF),
            pltpu.VMEM((128, 128), BF),
            pltpu.VMEM((2, TOK, 128), BF),
            pltpu.VMEM((2, 2, TOK, 128), BF),
            pltpu.VMEM((2, TOK, 128), BF),
            pltpu.VMEM((2, 2, TOK, 128), BF),
            pltpu.VMEM((3, 128, TOK), BF),
            pltpu.VMEM((3, 128, TOK * NBLK), BF),
            pltpu.VMEM((224, 256), BF),
            pltpu.VMEM((256, 224), BF),
            pltpu.VMEM((2, 2, TOK, HALF), BF),
            pltpu.VMEM((2, 2, XROWS, 2 * WIDE), BF),
            pltpu.VMEM((7, 16, 2 * WIDE), BF),
            pltpu.VMEM((2, 7, 16, WIDE), BF),
            pltpu.VMEM((XROWS, HID), BF),
            pltpu.VMEM((224, 256), BF),
            pltpu.VMEM((2, ROWS, 2 * WIDE), BF),
            pltpu.VMEM((2, 2, 4, 64, WIDE), BF),
            pltpu.VMEM((7, 16, 2 * WIDE), BF),
            pltpu.VMEM((2, 7, 16, WIDE), BF),
            pltpu.VMEM((2, 8, 16, 2 * WIDE), BF),
            pltpu.VMEM((2, 2, 8, 16, WIDE), BF),
            pltpu.VMEM((2, TOK, HALF), BF),
            pltpu.VMEM((2, 2, TOK, HALF), BF),
            pltpu.VMEM((TOK, D), F32),
            dma((2,)),
            dma, dma,
            dma, dma((2,)),
            dma, dma((2, 2)),
            dma, dma((2, 8)),
            dma, dma((2, 16)),
            dma, dma((2, 2)),
            dma, dma((2, 8)),
            dma, dma((2, 2)),
            dma, dma((2, 2)),
            dma, dma((2, 2)),
            dma, dma((2,)),
        ],
        compiler_params=pltpu.CompilerParams(
            collective_id=0, has_side_effects=True, vmem_limit_bytes=60 << 20
        ),
        name="relay",
    )(order, batches, gains, router[0].T, jnp.swapaxes(routes[0], 1, 2), caps, w_in[0], w_down[0])
    return out[None]


def solution(mesh):
    placed = (
        P(None, "expert", None),
        P(),
        P("section", None),
        P("section", None, None),
        P("section", None, "expert", None),
        P("section", None),
        P("section", None, None, "expert"),
        P("section", "expert", None),
    )
    return jax.shard_map(
        local,
        mesh=mesh,
        in_specs=placed,
        out_specs=P("section", None, "expert", None),
        check_vma=False,
    )
```

```python
import jax
import jax.numpy as jnp
from jax import lax
from jax.experimental import pallas as pl
from jax.experimental.pallas import tpu as pltpu
from jax.sharding import PartitionSpec as P

MESH = pl.DeviceIdType.MESH
BF, F32, I32 = jnp.bfloat16, jnp.float32, jnp.int32

D = 3584
EXPERTS = 8
HALF = D // 2
BLK = 256
NBLK = HALF // BLK
WIDE = HALF + BLK
TOK = 64
HID = 512
ROWS = 256
XROWS = 288
LOST = 99.0


def iota(shape, dim):
    return lax.broadcasted_iota(I32, shape, dim)


def nt(a, b):
    return lax.dot_general(a, b, (((1,), (1,)), ((), ())), preferred_element_type=F32)


def mm(a, b):
    return jnp.dot(a, b, preferred_element_type=F32)


def kernel(
    order_ref, batches_ref, gain_ref, router_ref, routes_ref, caps_ref, w_in_hbm, w_down_hbm, out_ref,
    w_in, w_down, u_buf, normed, onehot, rk_own, rk_near, gates_own, gates_near, pick_main, pick_ext, sel, pack,
    nb, x_buf, sa, sb, hidden, ext_out, out_buf, part, sa2, sn2, ra2, rn2, s3, r3, total_out,
    w_sem, rk_send, rk_recv, g_send, g_recv, nb_send, nb_recv, a1_send, a1_recv, b_send, b_recv, a2_send, a2_recv,
    part_send, part_recv, ra2_send, ra2_recv, rn2_send, rn2_recv, r3_send, r3_recv, u_send, u_recv,
):
    s, me = lax.axis_index("section"), lax.axis_index("expert")
    x, z, y = me // 16, lax.rem(me // 4, 4), lax.rem(me, 4)
    outer = jnp.logical_or(s == 0, s == 3)

    def chip(dx, dz, dy):
        return (s, lax.rem(x + dx, 2) * 16 + lax.rem(z + dz + 4, 4) * 4 + lax.rem(y + dy, 4))

    def send(src, dst, ssem, rsem, to):
        pltpu.make_async_remote_copy(
            src_ref=src, dst_ref=dst, send_sem=ssem, recv_sem=rsem, device_id=to, device_id_type=MESH
        ).start()

    def got(ref, sem):
        pltpu.make_async_remote_copy(
            src_ref=ref, dst_ref=ref, send_sem=sem, recv_sem=sem, device_id=chip(0, 0, 1), device_id_type=MESH
        ).wait_recv()

    def sent(ref, sem):
        pltpu.make_async_remote_copy(
            src_ref=ref, dst_ref=ref, send_sem=sem, recv_sem=sem, device_id=chip(0, 0, 1), device_id_type=MESH
        ).wait_send()

    offs = [(j % 2, (j // 2) * 2 + c) for c in range(2) for j in range(4)]
    toward, near = (1, 3), (3, 1)

    def lanes(p):
        return slice(p * WIDE, (p + 1) * WIDE)

    copy_in = pltpu.make_async_copy(w_in_hbm, w_in, w_sem.at[0])
    copy_down = pltpu.make_async_copy(w_down_hbm, w_down, w_sem.at[1])
    copy_in.start()
    copy_down.start()

    barrier = pltpu.get_barrier_semaphore()
    for dx, dz in offs[1:]:
        pl.semaphore_signal(barrier, inc=1, device_id=chip(dx, dz, 0), device_id_type=MESH)
    for m in (1, 3):
        pl.semaphore_signal(barrier, inc=1, device_id=chip(0, 0, m), device_id_type=MESH)
    for ds in (1, 3):
        pl.semaphore_signal(barrier, inc=1, device_id=(lax.rem(s + ds, 4), me), device_id_type=MESH)

    row, lane = iota((128, 128), 0), iota((128, 128), 1)
    o = row // 16
    dz_of = lax.rem(o // 2, 2) * 2 + o // 4
    expert_of = lax.rem(x + lax.rem(o, 2), 2) * 4 + lax.rem(z + dz_of, 4)
    onehot[...] = (lane == expert_of).astype(BF)
    r, c = iota((224, 256), 0), iota((224, 256), 1)
    sel[...] = (c == lax.rem(r, 32) * 8 + r // 32).astype(BF)
    r, c = iota((256, 224), 0), iota((256, 224), 1)
    pack[...] = (r == lax.rem(c, 32) * 8 + c // 32).astype(BF)
    lower = (iota((TOK, TOK), 0) > iota((TOK, TOK), 1)).astype(BF)
    eye = (iota((TOK, TOK), 0) == iota((TOK, TOK), 1)).astype(BF)
    gates_own[...] = jnp.zeros_like(gates_own)
    rk_own[...] = jnp.zeros_like(rk_own)

    def named(step):
        direction = jnp.where(s < 2, step, 1 - step)
        pair = routes_ref[direction]
        number = iota((EXPERTS, TOK), 0)
        names = jnp.logical_or(pair[0:1] == number, pair[1:2] == number)
        return names.astype(F32).astype(BF)

    for step in range(2):
        names = named(step)
        rank = nt(lower, names)
        kept = jnp.logical_and(nt(eye, names) > 0.5, rank < caps_ref[...].astype(F32))
        rk_own[step, :, 0:EXPERTS] = jnp.where(kept, rank, LOST).astype(BF)

    @pl.when(outer)
    def _():
        u_buf[0] = batches_ref[order_ref[jnp.where(s == 0, 0, 1)]]

    pl.semaphore_wait(barrier, 11)
    for p in range(2):
        send(rk_own, rk_near.at[p], rk_send, rk_recv, chip(0, 0, toward[p]))

    def layer(step, carry):
        direction = jnp.where(s < 2, step, 1 - step)

        def packer(ranks):
            rt = nt(onehot[...], ranks)
            main = (rt == lax.rem(iota((128, TOK), 0), 16).astype(F32)).astype(BF)
            rt7 = nt(onehot[...], jnp.concatenate([ranks] * NBLK, axis=0))
            rw, cl = iota((128, TOK * NBLK), 0), iota((128, TOK * NBLK), 1)
            want = (16 + lax.rem(rw, 16) // 8).astype(F32)
            ext = jnp.logical_and(rt7 == want, lax.rem(rw, 8) == cl // TOK).astype(BF)
            return main, ext

        pick_main[0], pick_ext[0] = packer(rk_own[step])

        def tables_near(p, carry):
            pick_main[p + 1], pick_ext[p + 1] = packer(rk_near[p, step])
            return carry

        first = jnp.logical_and(step == 0, outer)

        @pl.when(jnp.logical_and(step == 0, jnp.logical_not(outer)))
        def _():
            got(rk_near, rk_recv)

        @pl.when(jnp.logical_not(first))
        def _():
            lax.fori_loop(0, 2, tables_near, 0)

        @pl.when(jnp.logical_not(jnp.logical_and(step == 0, outer)))
        def _():
            got(u_buf.at[step], u_recv.at[step])

        total = jnp.zeros((TOK, 512), F32)
        for i in range(D // 512):
            v = u_buf[step, :, i * 512:(i + 1) * 512].astype(F32)
            total = total + v * v
        inv = lax.rsqrt(jnp.sum(total, axis=1, keepdims=True) * (1.0 / D) + 1e-06)
        for p in range(2):
            for i in range(p * HALF, (p + 1) * HALF, 256):
                v = u_buf[step, :, i:i + 256].astype(F32)
                normed[:, i:i + 256] = (v * inv * gain_ref[:, i:i + 256]).astype(BF)
            send(
                normed.at[:, p * HALF:(p + 1) * HALF], nb.at[step, p],
                nb_send, nb_recv.at[step, p], chip(0, 0, toward[p]),
            )

        def packed(which, source, put):
            main, ext = pick_main[which], pick_ext[which]
            for i in range(NBLK):
                put(i * BLK, mm(main, source(i)).astype(BF))
            stack = jnp.concatenate([source(i) for i in range(NBLK)], axis=0)
            put(HALF, mm(ext, stack).astype(BF))

        def send_own(i):
            (dx, dz), ch, j = offs[i], i // 4, i % 4
            send(sa.at[i - 1], x_buf.at[step, ch, j * 16:j * 16 + 16], a1_send, a1_recv.at[step, i], chip(dx, dz, 0))

        def send_near(p, i):
            (dx, dz), ch, at = offs[i], i // 4, near[p] * 64 + i % 4 * 16
            send(
                sb.at[p, i - 1], x_buf.at[step, ch, at:at + 16, lanes(p)],
                b_send, b_recv.at[step, p * 8 + i], chip(dx, dz, 0),
            )

        def forward_own(i):
            ch, j = i // 4, i % 4
            if i:
                got(x_buf.at[step, ch, j * 16:j * 16 + 16], a1_recv.at[step, i])
            for p in range(2):
                at = toward[p] * 64 + j * 16
                send(
                    x_buf.at[step, ch, j * 16:j * 16 + 16, lanes(p)], x_buf.at[step, ch, at:at + 16, lanes(p)],
                    a2_send, a2_recv.at[step, ch], chip(0, 0, near[p]),
                )

        def forward_near(p, i):
            ch, j = i // 4, i % 4
            at, to = near[p] * 64 + j * 16, 128 + j * 16
            if i:
                got(x_buf.at[step, ch, at:at + 16, lanes(p)], b_recv.at[step, p * 8 + i])
            send(
                x_buf.at[step, ch, at:at + 16, lanes(p)], x_buf.at[step, ch, to:to + 16, lanes(p)],
                a2_send, a2_recv.at[step, ch], chip(0, 0, toward[p]),
            )

        for p in range(2):
            def put_own(at, v):
                x_buf[step, 0, 0:16, p * WIDE + at:p * WIDE + at + BLK] = v[0:16]
                sa[:, :, p * WIDE + at:p * WIDE + at + BLK] = v[16:128].reshape(7, 16, BLK)

            packed(0, lambda i: normed[:, p * HALF + i * BLK:p * HALF + (i + 1) * BLK], put_own)
        for i in range(1, 8):
            send_own(i)
        forward_own(0)

        router = router_ref[...]
        high = router.astype(BF)
        low = (router - high.astype(F32)).astype(BF)
        scores = jax.nn.sigmoid(nt(normed[...], high) + nt(normed[...], low))
        chosen = jnp.sum(nt(eye, named(step)) * scores, axis=1, keepdims=True)
        gates_own[step, :, 0:EXPERTS] = (2.5 * scores / chosen).astype(BF)
        for p in range(2):
            send(gates_own.at[step], gates_near.at[step, p], g_send, g_recv.at[step], chip(0, 0, toward[p]))

        @pl.when(first)
        def _():
            got(rk_near, rk_recv)
            lax.fori_loop(0, 2, tables_near, 0)

        for p in range(2):
            def put_near(at, v):
                at_row = near[p] * 64
                x_buf[step, 0, at_row:at_row + 16, p * WIDE + at:p * WIDE + at + BLK] = v[0:16]
                sb[p, :, :, at:at + BLK] = v[16:128].reshape(7, 16, BLK)

            got(nb.at[step, p], nb_recv.at[step, p])
            packed(p + 1, lambda i: nb[step, p, :, i * BLK:(i + 1) * BLK], put_near)
            for i in (1, 2, 3):
                send_near(p, i)
            forward_near(p, 0)
        for i in range(4, 8):
            for p in range(2):
                send_near(p, i)
        for i in range(1, 8):
            forward_own(i)

        for p in range(2):
            for i in (1, 2, 3):
                forward_near(p, i)
        for i in range(4, 8):
            for p in range(2):
                forward_near(p, i)

        @pl.when(step == 0)
        def _():
            copy_in.wait()
            copy_down.wait()

        def arrived(ch):
            got(x_buf.at[step, ch, 0:ROWS, 0:WIDE], a2_recv.at[step, ch])
            for p in range(2):
                spread = mm(sel[...], x_buf[step, ch, 0:ROWS, p * WIDE + HALF:(p + 1) * WIDE]).astype(BF)
                for i in range(NBLK):
                    cols = slice(p * WIDE + i * BLK, p * WIDE + (i + 1) * BLK)
                    x_buf[step, ch, ROWS:XROWS, cols] = spread[i * 32:(i + 1) * 32]

        def up(ch, n):
            cols = slice(n * 256, (n + 1) * 256)
            g, v = (
                mm(x_buf[step, ch, :, 0:HALF], w_in[q, 0:HALF, cols])
                + mm(x_buf[step, ch, :, WIDE:WIDE + HALF], w_in[q, HALF:D, cols])
                for q in range(2)
            )
            hidden[:, cols] = (jax.nn.silu(g) * v).astype(BF)

        def down(ch, p):
            for n in range(NBLK):
                v = mm(hidden[...], w_down[:, p * HALF + n * BLK:p * HALF + (n + 1) * BLK]).astype(BF)
                out_buf[ch, 0:ROWS, p * WIDE + n * BLK:p * WIDE + (n + 1) * BLK] = v[0:ROWS]
                ext_out[n * 32:(n + 1) * 32, :] = v[ROWS:XROWS]
            out_buf[ch, 0:ROWS, p * WIDE + HALF:(p + 1) * WIDE] = mm(pack[...], ext_out[...]).astype(BF)

        def send_part(ch, p, q):
            first, to = (128, near[p]) if q else (toward[p] * 64, toward[p])
            send(
                out_buf.at[ch, first:first + 64, lanes(p)], part.at[step, ch, p * 2 + q],
                part_send, part_recv.at[step, ch * 4 + p * 2 + q], chip(0, 0, to),
            )

        def back(ch, p, q):
            got(part.at[step, ch, p * 2 + q], part_recv.at[step, ch * 4 + p * 2 + q])
            for j in range(4):
                i = ch * 4 + j
                dx, dz = offs[i]
                first = near[p] * 64 * q + j * 16
                v = out_buf[ch, first:first + 16, lanes(p)].astype(F32)
                v = (v + part[step, ch, p * 2 + q, j * 16:j * 16 + 16].astype(F32)).astype(BF)
                if q and i:
                    sn2[p, i - 1] = v
                    send(sn2.at[p, i - 1], rn2.at[step, p, i], rn2_send, rn2_recv.at[step, p], chip(dx, -dz, 0))
                elif q:
                    rn2[step, p, 0] = v
                elif i:
                    sa2[i - 1, :, lanes(p)] = v
                    send(
                        sa2.at[i - 1, :, lanes(p)], ra2.at[step, i, :, lanes(p)],
                        ra2_send, ra2_recv.at[step, p], chip(dx, -dz, 0),
                    )
                else:
                    ra2[step, 0, :, lanes(p)] = v

        arrived(0)
        up(0, 0)
        up(0, 1)
        for p in range(2):
            down(0, p)
            send_part(0, p, 1)
            send_part(0, p, 0)
        arrived(1)
        up(1, 0)
        up(1, 1)
        down(1, 0)
        send_part(1, 0, 1)
        down(1, 1)
        send_part(1, 1, 1)
        back(0, 0, 1)
        back(0, 1, 1)
        send_part(1, 0, 0)
        send_part(1, 1, 0)
        back(0, 0, 0)
        back(0, 1, 0)
        for q in (1, 0):
            for p in range(2):
                back(1, p, q)

        def weights(ranks, gate):
            rt, gt = nt(ranks, onehot[...]), nt(gate, onehot[...])
            main = jnp.where(rt == lax.rem(iota((TOK, 128), 1), 16).astype(F32), gt, 0.0).astype(BF)
            rw, cl = iota((TOK * NBLK, 128), 0), iota((TOK * NBLK, 128), 1)
            want = (16 + lax.rem(cl, 16) // 8).astype(F32)
            take = jnp.logical_and(
                jnp.concatenate([rt] * NBLK, axis=0) == want, lax.rem(cl, 8) == rw // TOK
            )
            return main, jnp.where(take, jnp.concatenate([gt] * NBLK, axis=0), 0.0).astype(BF)

        def weighed(tables, source, put):
            main, ext = tables
            over = mm(ext, source(HALF))
            for i in range(NBLK):
                put(i * BLK, mm(main, source(i * BLK)) + over[i * TOK:(i + 1) * TOK])

        got(gates_near.at[step], g_recv.at[step])
        for p in range(2):
            def put_back(at, v):
                s3[p, :, at:at + BLK] = v.astype(BF)

            tables = weights(rk_near[p, step], gates_near[step, p])
            got(rn2.at[step, p, 1:8], rn2_recv.at[step, p])
            weighed(tables, lambda at: rn2[step, p, :, :, at:at + BLK].reshape(128, BLK), put_back)
            send(s3.at[p], r3.at[step, p], r3_send, r3_recv.at[step, p], chip(0, 0, near[p]))

        tables = weights(rk_own[step], gates_own[step])
        for p in range(2):
            got(ra2.at[step, 1:8, :, lanes(p)], ra2_recv.at[step, p])

            def put_sum(at, v):
                cols = slice(p * HALF + at, p * HALF + at + BLK)
                total_out[:, cols] = u_buf[step, :, cols].astype(F32) + v

            weighed(tables, lambda at: ra2[step, :, :, p * WIDE + at:p * WIDE + at + BLK].reshape(128, BLK), put_sum)

        target = jnp.where(direction == 0, s + 1, s - 1)
        relays = jnp.logical_and(target >= 0, target <= 3)
        target_step = jnp.where(jnp.logical_and(step == 0, outer), 0, 1)
        for p in range(2):
            got(r3.at[step, p], r3_recv.at[step, p])
            half = slice(p * HALF, (p + 1) * HALF)
            for i in range(NBLK):
                cols = slice(p * HALF + i * BLK, p * HALF + (i + 1) * BLK)
                v = total_out[:, cols] + r3[step, p, :, i * BLK:(i + 1) * BLK].astype(F32)
                out_ref[direction, :, cols] = v.astype(BF)

            @pl.when(relays)
            def _():
                send(
                    out_ref.at[direction, :, half], u_buf.at[target_step, :, half],
                    u_send, u_recv.at[target_step], (target, me),
                )

        sent(nb.at[step], nb_send)
        sent(sa, a1_send)
        sent(sb, b_send)
        sent(x_buf.at[step, :, 0:ROWS, 0:WIDE], a2_send)
        sent(gates_near.at[step], g_send)
        sent(part.at[step], part_send)
        sent(sa2, ra2_send)
        sent(sn2, rn2_send)
        sent(s3, r3_send)

        @pl.when(relays)
        def _():
            sent(u_buf.at[step], u_send)

        return carry

    lax.fori_loop(0, 2, layer, 0)
    sent(rk_near, rk_send)


def local(batches, order, gains, router, routes, caps, w_in, w_down):
    vmem, hbm = pl.BlockSpec(memory_space=pltpu.VMEM), pl.BlockSpec(memory_space=pl.ANY)
    dma = pltpu.SemaphoreType.DMA
    out = pl.pallas_call(
        kernel,
        out_shape=jax.ShapeDtypeStruct((2, TOK, D), BF),
        in_specs=[pl.BlockSpec(memory_space=pltpu.SMEM), vmem, vmem, vmem, vmem, vmem, hbm, hbm],
        out_specs=vmem,
        scratch_shapes=[
            pltpu.VMEM((2, D, HID), BF),
            pltpu.VMEM((HID, D), BF),
            pltpu.VMEM((2, TOK, D), BF),
            pltpu.VMEM((TOK, D), BF),
            pltpu.VMEM((128, 128), BF),
            pltpu.VMEM((2, TOK, 128), BF),
            pltpu.VMEM((2, 2, TOK, 128), BF),
            pltpu.VMEM((2, TOK, 128), BF),
            pltpu.VMEM((2, 2, TOK, 128), BF),
            pltpu.VMEM((3, 128, TOK), BF),
            pltpu.VMEM((3, 128, TOK * NBLK), BF),
            pltpu.VMEM((224, 256), BF),
            pltpu.VMEM((256, 224), BF),
            pltpu.VMEM((2, 2, TOK, HALF), BF),
            pltpu.VMEM((2, 2, XROWS, 2 * WIDE), BF),
            pltpu.VMEM((7, 16, 2 * WIDE), BF),
            pltpu.VMEM((2, 7, 16, WIDE), BF),
            pltpu.VMEM((XROWS, HID), BF),
            pltpu.VMEM((224, 256), BF),
            pltpu.VMEM((2, ROWS, 2 * WIDE), BF),
            pltpu.VMEM((2, 2, 4, 64, WIDE), BF),
            pltpu.VMEM((7, 16, 2 * WIDE), BF),
            pltpu.VMEM((2, 7, 16, WIDE), BF),
            pltpu.VMEM((2, 8, 16, 2 * WIDE), BF),
            pltpu.VMEM((2, 2, 8, 16, WIDE), BF),
            pltpu.VMEM((2, TOK, HALF), BF),
            pltpu.VMEM((2, 2, TOK, HALF), BF),
            pltpu.VMEM((TOK, D), F32),
            dma((2,)),
            dma, dma,
            dma, dma((2,)),
            dma, dma((2, 2)),
            dma, dma((2, 8)),
            dma, dma((2, 16)),
            dma, dma((2, 2)),
            dma, dma((2, 8)),
            dma, dma((2, 2)),
            dma, dma((2, 2)),
            dma, dma((2, 2)),
            dma, dma((2,)),
        ],
        compiler_params=pltpu.CompilerParams(
            collective_id=0, has_side_effects=True, vmem_limit_bytes=60 << 20
        ),
        name="relay",
    )(order, batches, gains, router[0].T, jnp.swapaxes(routes[0], 1, 2), caps, w_in[0], w_down[0])
    return out[None]


def solution(mesh):
    placed = (
        P(None, "expert", None),
        P(),
        P("section", None),
        P("section", None, None),
        P("section", None, "expert", None),
        P("section", None),
        P("section", None, None, "expert"),
        P("section", "expert", None),
    )
    return jax.shard_map(
        local,
        mesh=mesh,
        in_specs=placed,
        out_specs=P("section", None, "expert", None),
        check_vma=False,
    )
```

```python
import jax
import jax.numpy as jnp
from jax import lax
from jax.experimental import pallas as pl
from jax.experimental.pallas import tpu as pltpu
from jax.sharding import PartitionSpec as P

MESH = pl.DeviceIdType.MESH
BF, F32, I32 = jnp.bfloat16, jnp.float32, jnp.int32

D = 3584
EXPERTS = 8
HALF = D // 2
BLK = 256
NBLK = HALF // BLK
WIDE = HALF + BLK
TOK = 64
HID = 512
ROWS = 256
XROWS = 288
LOST = 99.0


def iota(shape, dim):
    return lax.broadcasted_iota(I32, shape, dim)


def nt(a, b):
    return lax.dot_general(a, b, (((1,), (1,)), ((), ())), preferred_element_type=F32)


def mm(a, b):
    return jnp.dot(a, b, preferred_element_type=F32)


def kernel(
    order_ref, batches_ref, gain_ref, router_ref, routes_ref, caps_ref, w_in_hbm, w_down_hbm, out_ref,
    w_in, w_down, u_buf, normed, onehot, rk_own, rk_near, gates_own, gates_near, pick_main, pick_ext, sel, pack,
    nb, x_buf, sa, sb, hidden, ext_out, out_buf, part, sa2, sn2, ra2, rn2, s3, r3, total_out, gate_main, gate_ext,
    w_sem, rk_send, rk_recv, g_send, g_recv, nb_send, nb_recv, a1_send, a1_recv, b_send, b_recv, a2_send, a2_recv,
    part_send, part_recv, ra2_send, ra2_recv, rn2_send, rn2_recv, r3_send, r3_recv, u_send, u_recv,
):
    s, me = lax.axis_index("section"), lax.axis_index("expert")
    x, z, y = me // 16, lax.rem(me // 4, 4), lax.rem(me, 4)
    outer = jnp.logical_or(s == 0, s == 3)

    def chip(dx, dz, dy):
        return (s, lax.rem(x + dx, 2) * 16 + lax.rem(z + dz + 4, 4) * 4 + lax.rem(y + dy, 4))

    def send(src, dst, ssem, rsem, to):
        pltpu.make_async_remote_copy(
            src_ref=src, dst_ref=dst, send_sem=ssem, recv_sem=rsem, device_id=to, device_id_type=MESH
        ).start()

    def got(ref, sem):
        pltpu.make_async_remote_copy(
            src_ref=ref, dst_ref=ref, send_sem=sem, recv_sem=sem, device_id=chip(0, 0, 1), device_id_type=MESH
        ).wait_recv()

    def sent(ref, sem):
        pltpu.make_async_remote_copy(
            src_ref=ref, dst_ref=ref, send_sem=sem, recv_sem=sem, device_id=chip(0, 0, 1), device_id_type=MESH
        ).wait_send()

    offs = [(j % 2, (j // 2) * 2 + c) for c in range(2) for j in range(4)]
    toward, near = (1, 3), (3, 1)

    def lanes(p):
        return slice(p * WIDE, (p + 1) * WIDE)

    copy_in = pltpu.make_async_copy(w_in_hbm, w_in, w_sem.at[0])
    copy_down = pltpu.make_async_copy(w_down_hbm, w_down, w_sem.at[1])
    copy_in.start()
    copy_down.start()

    barrier = pltpu.get_barrier_semaphore()
    for dx, dz in offs[1:]:
        pl.semaphore_signal(barrier, inc=1, device_id=chip(dx, dz, 0), device_id_type=MESH)
    for m in (1, 3):
        pl.semaphore_signal(barrier, inc=1, device_id=chip(0, 0, m), device_id_type=MESH)
    for ds in (1, 3):
        pl.semaphore_signal(barrier, inc=1, device_id=(lax.rem(s + ds, 4), me), device_id_type=MESH)

    row, lane = iota((128, 128), 0), iota((128, 128), 1)
    o = row // 16
    dz_of = lax.rem(o // 2, 2) * 2 + o // 4
    expert_of = lax.rem(x + lax.rem(o, 2), 2) * 4 + lax.rem(z + dz_of, 4)
    onehot[...] = (lane == expert_of).astype(BF)
    r, c = iota((224, 256), 0), iota((224, 256), 1)
    sel[...] = (c == lax.rem(r, 32) * 8 + r // 32).astype(BF)
    r, c = iota((256, 224), 0), iota((256, 224), 1)
    pack[...] = (r == lax.rem(c, 32) * 8 + c // 32).astype(BF)
    lower = (iota((TOK, TOK), 0) > iota((TOK, TOK), 1)).astype(BF)
    eye = (iota((TOK, TOK), 0) == iota((TOK, TOK), 1)).astype(BF)
    gates_own[...] = jnp.zeros_like(gates_own)
    rk_own[...] = jnp.zeros_like(rk_own)

    def named(step):
        direction = jnp.where(s < 2, step, 1 - step)
        pair = routes_ref[direction]
        number = iota((EXPERTS, TOK), 0)
        names = jnp.logical_or(pair[0:1] == number, pair[1:2] == number)
        return names.astype(F32).astype(BF)

    for step in range(2):
        names = named(step)
        rank = nt(lower, names)
        kept = jnp.logical_and(nt(eye, names) > 0.5, rank < caps_ref[...].astype(F32))
        rk_own[step, :, 0:EXPERTS] = jnp.where(kept, rank, LOST).astype(BF)

    @pl.when(outer)
    def _():
        u_buf[0] = batches_ref[order_ref[jnp.where(s == 0, 0, 1)]]

    pl.semaphore_wait(barrier, 11)
    for p in range(2):
        send(rk_own, rk_near.at[p], rk_send, rk_recv, chip(0, 0, toward[p]))

    def layer(step, carry):
        direction = jnp.where(s < 2, step, 1 - step)

        def packer(ranks):
            rt = nt(onehot[...], ranks)
            main = (rt == lax.rem(iota((128, TOK), 0), 16).astype(F32)).astype(BF)
            rt7 = nt(onehot[...], jnp.concatenate([ranks] * NBLK, axis=0))
            rw, cl = iota((128, TOK * NBLK), 0), iota((128, TOK * NBLK), 1)
            want = (16 + lax.rem(rw, 16) // 8).astype(F32)
            ext = jnp.logical_and(rt7 == want, lax.rem(rw, 8) == cl // TOK).astype(BF)
            return main, ext

        pick_main[0], pick_ext[0] = packer(rk_own[step])

        def tables_near(p, carry):
            pick_main[p + 1], pick_ext[p + 1] = packer(rk_near[p, step])
            return carry

        first = jnp.logical_and(step == 0, outer)

        @pl.when(jnp.logical_and(step == 0, jnp.logical_not(outer)))
        def _():
            got(rk_near, rk_recv)

        @pl.when(jnp.logical_not(first))
        def _():
            lax.fori_loop(0, 2, tables_near, 0)

        @pl.when(jnp.logical_not(jnp.logical_and(step == 0, outer)))
        def _():
            got(u_buf.at[step], u_recv.at[step])

        total = jnp.zeros((TOK, 512), F32)
        for i in range(D // 512):
            v = u_buf[step, :, i * 512:(i + 1) * 512].astype(F32)
            total = total + v * v
        inv = lax.rsqrt(jnp.sum(total, axis=1, keepdims=True) * (1.0 / D) + 1e-06)
        for p in range(2):
            for i in range(p * HALF, (p + 1) * HALF, 256):
                v = u_buf[step, :, i:i + 256].astype(F32)
                normed[:, i:i + 256] = (v * inv * gain_ref[:, i:i + 256]).astype(BF)
            send(
                normed.at[:, p * HALF:(p + 1) * HALF], nb.at[step, p],
                nb_send, nb_recv.at[step, p], chip(0, 0, toward[p]),
            )

        def packed(which, source, put):
            main, ext = pick_main[which], pick_ext[which]
            for i in range(NBLK):
                put(i * BLK, mm(main, source(i)).astype(BF))
            stack = jnp.concatenate([source(i) for i in range(NBLK)], axis=0)
            put(HALF, mm(ext, stack).astype(BF))

        def send_own(i):
            (dx, dz), ch, j = offs[i], i // 4, i % 4
            send(sa.at[i - 1], x_buf.at[step, ch, j * 16:j * 16 + 16], a1_send, a1_recv.at[step, i], chip(dx, dz, 0))

        def send_near(p, i):
            (dx, dz), ch, at = offs[i], i // 4, near[p] * 64 + i % 4 * 16
            send(
                sb.at[p, i - 1], x_buf.at[step, ch, at:at + 16, lanes(p)],
                b_send, b_recv.at[step, p * 8 + i], chip(dx, dz, 0),
            )

        def forward_own(i):
            ch, j = i // 4, i % 4
            if i:
                got(x_buf.at[step, ch, j * 16:j * 16 + 16], a1_recv.at[step, i])
            for p in range(2):
                at = toward[p] * 64 + j * 16
                send(
                    x_buf.at[step, ch, j * 16:j * 16 + 16, lanes(p)], x_buf.at[step, ch, at:at + 16, lanes(p)],
                    a2_send, a2_recv.at[step, ch], chip(0, 0, near[p]),
                )

        def forward_near(p, i):
            ch, j = i // 4, i % 4
            at, to = near[p] * 64 + j * 16, 128 + j * 16
            if i:
                got(x_buf.at[step, ch, at:at + 16, lanes(p)], b_recv.at[step, p * 8 + i])
            send(
                x_buf.at[step, ch, at:at + 16, lanes(p)], x_buf.at[step, ch, to:to + 16, lanes(p)],
                a2_send, a2_recv.at[step, ch], chip(0, 0, toward[p]),
            )

        for p in range(2):
            def put_own(at, v):
                x_buf[step, 0, 0:16, p * WIDE + at:p * WIDE + at + BLK] = v[0:16]
                sa[:, :, p * WIDE + at:p * WIDE + at + BLK] = v[16:128].reshape(7, 16, BLK)

            packed(0, lambda i: normed[:, p * HALF + i * BLK:p * HALF + (i + 1) * BLK], put_own)
        for i in range(1, 8):
            send_own(i)
        forward_own(0)

        router = router_ref[...]
        high = router.astype(BF)
        low = (router - high.astype(F32)).astype(BF)
        scores = jax.nn.sigmoid(nt(normed[...], high) + nt(normed[...], low))
        chosen = jnp.sum(nt(eye, named(step)) * scores, axis=1, keepdims=True)
        gates_own[step, :, 0:EXPERTS] = (2.5 * scores / chosen).astype(BF)
        for p in range(2):
            send(gates_own.at[step], gates_near.at[step, p], g_send, g_recv.at[step], chip(0, 0, toward[p]))

        @pl.when(first)
        def _():
            got(rk_near, rk_recv)
            lax.fori_loop(0, 2, tables_near, 0)

        for p in range(2):
            def put_near(at, v):
                at_row = near[p] * 64
                x_buf[step, 0, at_row:at_row + 16, p * WIDE + at:p * WIDE + at + BLK] = v[0:16]
                sb[p, :, :, at:at + BLK] = v[16:128].reshape(7, 16, BLK)

            got(nb.at[step, p], nb_recv.at[step, p])
            packed(p + 1, lambda i: nb[step, p, :, i * BLK:(i + 1) * BLK], put_near)
            for i in (1, 2, 3):
                send_near(p, i)
            forward_near(p, 0)
        for i in range(4, 8):
            for p in range(2):
                send_near(p, i)
        for i in range(1, 8):
            forward_own(i)

        for p in range(2):
            for i in (1, 2, 3):
                forward_near(p, i)
        for i in range(4, 8):
            for p in range(2):
                forward_near(p, i)

        @pl.when(step == 0)
        def _():
            copy_in.wait()
            copy_down.wait()

        def arrived(ch):
            got(x_buf.at[step, ch, 0:ROWS, 0:WIDE], a2_recv.at[step, ch])
            for p in range(2):
                spread = mm(sel[...], x_buf[step, ch, 0:ROWS, p * WIDE + HALF:(p + 1) * WIDE]).astype(BF)
                for i in range(NBLK):
                    cols = slice(p * WIDE + i * BLK, p * WIDE + (i + 1) * BLK)
                    x_buf[step, ch, ROWS:XROWS, cols] = spread[i * 32:(i + 1) * 32]

        def up(ch, n):
            cols = slice(n * 256, (n + 1) * 256)
            g, v = (
                mm(x_buf[step, ch, :, 0:HALF], w_in[q, 0:HALF, cols])
                + mm(x_buf[step, ch, :, WIDE:WIDE + HALF], w_in[q, HALF:D, cols])
                for q in range(2)
            )
            hidden[:, cols] = (jax.nn.silu(g) * v).astype(BF)

        def down(ch, p):
            for n in range(NBLK):
                v = mm(hidden[...], w_down[:, p * HALF + n * BLK:p * HALF + (n + 1) * BLK]).astype(BF)
                out_buf[ch, 0:ROWS, p * WIDE + n * BLK:p * WIDE + (n + 1) * BLK] = v[0:ROWS]
                ext_out[n * 32:(n + 1) * 32, :] = v[ROWS:XROWS]
            out_buf[ch, 0:ROWS, p * WIDE + HALF:(p + 1) * WIDE] = mm(pack[...], ext_out[...]).astype(BF)

        def send_part(ch, p, q):
            first, to = (128, near[p]) if q else (toward[p] * 64, toward[p])
            send(
                out_buf.at[ch, first:first + 64, lanes(p)], part.at[step, ch, p * 2 + q],
                part_send, part_recv.at[step, ch * 4 + p * 2 + q], chip(0, 0, to),
            )

        def back(ch, p, q):
            got(part.at[step, ch, p * 2 + q], part_recv.at[step, ch * 4 + p * 2 + q])
            for j in range(4):
                i = ch * 4 + j
                dx, dz = offs[i]
                first = near[p] * 64 * q + j * 16
                v = out_buf[ch, first:first + 16, lanes(p)].astype(F32)
                v = (v + part[step, ch, p * 2 + q, j * 16:j * 16 + 16].astype(F32)).astype(BF)
                if q and i:
                    sn2[p, i - 1] = v
                    send(sn2.at[p, i - 1], rn2.at[step, p, i], rn2_send, rn2_recv.at[step, p], chip(dx, -dz, 0))
                elif q:
                    rn2[step, p, 0] = v
                elif i:
                    sa2[i - 1, :, lanes(p)] = v
                    send(
                        sa2.at[i - 1, :, lanes(p)], ra2.at[step, i, :, lanes(p)],
                        ra2_send, ra2_recv.at[step, p], chip(dx, -dz, 0),
                    )
                else:
                    ra2[step, 0, :, lanes(p)] = v

        def weights(ranks, gate):
            rt, gt = nt(ranks, onehot[...]), nt(gate, onehot[...])
            main = jnp.where(rt == lax.rem(iota((TOK, 128), 1), 16).astype(F32), gt, 0.0).astype(BF)
            rw, cl = iota((TOK * NBLK, 128), 0), iota((TOK * NBLK, 128), 1)
            want = (16 + lax.rem(cl, 16) // 8).astype(F32)
            take = jnp.logical_and(
                jnp.concatenate([rt] * NBLK, axis=0) == want, lax.rem(cl, 8) == rw // TOK
            )
            return main, jnp.where(take, jnp.concatenate([gt] * NBLK, axis=0), 0.0).astype(BF)

        got(gates_near.at[step], g_recv.at[step])
        for p in range(2):
            gate_main[p], gate_ext[p] = weights(rk_near[p, step], gates_near[step, p])
        gate_main[2], gate_ext[2] = weights(rk_own[step], gates_own[step])

        arrived(0)
        up(0, 0)
        up(0, 1)
        for p in range(2):
            down(0, p)
            send_part(0, p, 1)
            send_part(0, p, 0)
        arrived(1)
        up(1, 0)
        up(1, 1)
        down(1, 0)
        send_part(1, 0, 1)
        down(1, 1)
        send_part(1, 1, 1)
        back(0, 0, 1)
        back(0, 1, 1)
        send_part(1, 0, 0)
        send_part(1, 1, 0)
        back(0, 0, 0)
        back(0, 1, 0)
        for q in (1, 0):
            for p in range(2):
                back(1, p, q)

        def weighed(tables, source, put):
            main, ext = tables
            over = mm(ext, source(HALF))
            for i in range(NBLK):
                put(i * BLK, mm(main, source(i * BLK)) + over[i * TOK:(i + 1) * TOK])

        cuts = slice(0, 4 * BLK), slice(4 * BLK, HALF)

        for p in range(2):
            def put_back(at, v):
                s3[p, :, at:at + BLK] = v.astype(BF)

            tables = gate_main[p], gate_ext[p]
            got(rn2.at[step, p, 1:8], rn2_recv.at[step, p])
            weighed(tables, lambda at: rn2[step, p, :, :, at:at + BLK].reshape(128, BLK), put_back)
            for h, cut in enumerate(cuts):
                send(s3.at[p, :, cut], r3.at[step, p, :, cut], r3_send, r3_recv.at[step, p * 2 + h], chip(0, 0, near[p]))

        tables = gate_main[2], gate_ext[2]
        for p in range(2):
            got(ra2.at[step, 1:8, :, lanes(p)], ra2_recv.at[step, p])

            def put_sum(at, v):
                cols = slice(p * HALF + at, p * HALF + at + BLK)
                total_out[:, cols] = u_buf[step, :, cols].astype(F32) + v

            weighed(tables, lambda at: ra2[step, :, :, p * WIDE + at:p * WIDE + at + BLK].reshape(128, BLK), put_sum)

        target = jnp.where(direction == 0, s + 1, s - 1)
        relays = jnp.logical_and(target >= 0, target <= 3)
        target_step = jnp.where(jnp.logical_and(step == 0, outer), 0, 1)
        for h, cut in enumerate(cuts):
            for p in range(2):
                got(r3.at[step, p, :, cut], r3_recv.at[step, p * 2 + h])
                for at in range(cut.start, cut.stop, BLK):
                    cols = slice(p * HALF + at, p * HALF + at + BLK)
                    v = total_out[:, cols] + r3[step, p, :, at:at + BLK].astype(F32)
                    out_ref[direction, :, cols] = v.astype(BF)
                half = slice(p * HALF + cut.start, p * HALF + cut.stop)

                @pl.when(relays)
                def _():
                    send(
                        out_ref.at[direction, :, half], u_buf.at[target_step, :, half],
                        u_send, u_recv.at[target_step], (target, me),
                    )

        sent(nb.at[step], nb_send)
        sent(sa, a1_send)
        sent(sb, b_send)
        sent(x_buf.at[step, :, 0:ROWS, 0:WIDE], a2_send)
        sent(gates_near.at[step], g_send)
        sent(part.at[step], part_send)
        sent(sa2, ra2_send)
        sent(sn2, rn2_send)
        sent(s3, r3_send)

        @pl.when(relays)
        def _():
            sent(u_buf.at[step], u_send)

        return carry

    lax.fori_loop(0, 2, layer, 0)
    sent(rk_near, rk_send)


def local(batches, order, gains, router, routes, caps, w_in, w_down):
    vmem, hbm = pl.BlockSpec(memory_space=pltpu.VMEM), pl.BlockSpec(memory_space=pl.ANY)
    dma = pltpu.SemaphoreType.DMA
    out = pl.pallas_call(
        kernel,
        out_shape=jax.ShapeDtypeStruct((2, TOK, D), BF),
        in_specs=[pl.BlockSpec(memory_space=pltpu.SMEM), vmem, vmem, vmem, vmem, vmem, hbm, hbm],
        out_specs=vmem,
        scratch_shapes=[
            pltpu.VMEM((2, D, HID), BF),
            pltpu.VMEM((HID, D), BF),
            pltpu.VMEM((2, TOK, D), BF),
            pltpu.VMEM((TOK, D), BF),
            pltpu.VMEM((128, 128), BF),
            pltpu.VMEM((2, TOK, 128), BF),
            pltpu.VMEM((2, 2, TOK, 128), BF),
            pltpu.VMEM((2, TOK, 128), BF),
            pltpu.VMEM((2, 2, TOK, 128), BF),
            pltpu.VMEM((3, 128, TOK), BF),
            pltpu.VMEM((3, 128, TOK * NBLK), BF),
            pltpu.VMEM((224, 256), BF),
            pltpu.VMEM((256, 224), BF),
            pltpu.VMEM((2, 2, TOK, HALF), BF),
            pltpu.VMEM((2, 2, XROWS, 2 * WIDE), BF),
            pltpu.VMEM((7, 16, 2 * WIDE), BF),
            pltpu.VMEM((2, 7, 16, WIDE), BF),
            pltpu.VMEM((XROWS, HID), BF),
            pltpu.VMEM((224, 256), BF),
            pltpu.VMEM((2, ROWS, 2 * WIDE), BF),
            pltpu.VMEM((2, 2, 4, 64, WIDE), BF),
            pltpu.VMEM((7, 16, 2 * WIDE), BF),
            pltpu.VMEM((2, 7, 16, WIDE), BF),
            pltpu.VMEM((2, 8, 16, 2 * WIDE), BF),
            pltpu.VMEM((2, 2, 8, 16, WIDE), BF),
            pltpu.VMEM((2, TOK, HALF), BF),
            pltpu.VMEM((2, 2, TOK, HALF), BF),
            pltpu.VMEM((TOK, D), F32),
            pltpu.VMEM((3, TOK, 128), BF),
            pltpu.VMEM((3, TOK * NBLK, 128), BF),
            dma((2,)),
            dma, dma,
            dma, dma((2,)),
            dma, dma((2, 2)),
            dma, dma((2, 8)),
            dma, dma((2, 16)),
            dma, dma((2, 2)),
            dma, dma((2, 8)),
            dma, dma((2, 2)),
            dma, dma((2, 2)),
            dma, dma((2, 4)),
            dma, dma((2,)),
        ],
        compiler_params=pltpu.CompilerParams(
            collective_id=0, has_side_effects=True, vmem_limit_bytes=60 << 20
        ),
        name="relay",
    )(order, batches, gains, router[0].T, jnp.swapaxes(routes[0], 1, 2), caps, w_in[0], w_down[0])
    return out[None]


def solution(mesh):
    placed = (
        P(None, "expert", None),
        P(),
        P("section", None),
        P("section", None, None),
        P("section", None, "expert", None),
        P("section", None),
        P("section", None, None, "expert"),
        P("section", "expert", None),
    )
    return jax.shard_map(
        local,
        mesh=mesh,
        in_specs=placed,
        out_specs=P("section", None, "expert", None),
        check_vma=False,
    )
```

```python
import jax
import jax.numpy as jnp
from jax import lax
from jax.experimental import pallas as pl
from jax.experimental.pallas import tpu as pltpu
from jax.sharding import PartitionSpec as P

MESH = pl.DeviceIdType.MESH
BF, F32, I32 = jnp.bfloat16, jnp.float32, jnp.int32

D = 3584
EXPERTS = 8
HALF = D // 2
BLK = 256
NBLK = HALF // BLK
WIDE = HALF + BLK
TOK = 64
HID = 512
ROWS = 256
XROWS = 288
LOST = 99.0


def iota(shape, dim):
    return lax.broadcasted_iota(I32, shape, dim)


def nt(a, b):
    return lax.dot_general(a, b, (((1,), (1,)), ((), ())), preferred_element_type=F32)


def mm(a, b):
    return jnp.dot(a, b, preferred_element_type=F32)


def kernel(
    order_ref, batches_ref, gain_ref, router_ref, routes_ref, caps_ref, w_in_hbm, w_down_hbm, out_ref,
    w_in, w_down, u_buf, normed, onehot, rk_own, rk_near, gates_own, gates_near, pick_main, pick_ext, sel, pack,
    nb, x_buf, sa, sb, hidden, ext_out, out_buf, part, sa2, sn2, ra2, rn2, s3, r3, total_out, gate_main, gate_ext,
    w_sem, rk_send, rk_recv, g_send, g_recv, nb_send, nb_recv, a1_send, a1_recv, b_send, b_recv, a2_send, a2_recv,
    part_send, part_recv, ra2_send, ra2_recv, rn2_send, rn2_recv, r3_send, r3_recv, u_send, u_recv,
):
    s, me = lax.axis_index("section"), lax.axis_index("expert")
    x, z, y = me // 16, lax.rem(me // 4, 4), lax.rem(me, 4)
    outer = jnp.logical_or(s == 0, s == 3)

    def chip(dx, dz, dy):
        return (s, lax.rem(x + dx, 2) * 16 + lax.rem(z + dz + 4, 4) * 4 + lax.rem(y + dy, 4))

    def send(src, dst, ssem, rsem, to):
        pltpu.make_async_remote_copy(
            src_ref=src, dst_ref=dst, send_sem=ssem, recv_sem=rsem, device_id=to, device_id_type=MESH
        ).start()

    def got(ref, sem):
        pltpu.make_async_remote_copy(
            src_ref=ref, dst_ref=ref, send_sem=sem, recv_sem=sem, device_id=chip(0, 0, 1), device_id_type=MESH
        ).wait_recv()

    def sent(ref, sem):
        pltpu.make_async_remote_copy(
            src_ref=ref, dst_ref=ref, send_sem=sem, recv_sem=sem, device_id=chip(0, 0, 1), device_id_type=MESH
        ).wait_send()

    offs = [(j % 2, (j // 2) * 2 + c) for c in range(2) for j in range(4)]
    toward, near = (1, 3), (3, 1)

    def lanes(p):
        return slice(p * WIDE, (p + 1) * WIDE)

    copy_in = pltpu.make_async_copy(w_in_hbm, w_in, w_sem.at[0])
    copy_down = pltpu.make_async_copy(w_down_hbm, w_down, w_sem.at[1])
    copy_in.start()
    copy_down.start()

    barrier = pltpu.get_barrier_semaphore()
    for dx, dz in offs[1:]:
        pl.semaphore_signal(barrier, inc=1, device_id=chip(dx, dz, 0), device_id_type=MESH)
    for m in (1, 3):
        pl.semaphore_signal(barrier, inc=1, device_id=chip(0, 0, m), device_id_type=MESH)
    for ds in (1, 3):
        pl.semaphore_signal(barrier, inc=1, device_id=(lax.rem(s + ds, 4), me), device_id_type=MESH)

    row, lane = iota((128, 128), 0), iota((128, 128), 1)
    o = row // 16
    dz_of = lax.rem(o // 2, 2) * 2 + o // 4
    expert_of = lax.rem(x + lax.rem(o, 2), 2) * 4 + lax.rem(z + dz_of, 4)
    onehot[...] = (lane == expert_of).astype(BF)
    r, c = iota((224, 256), 0), iota((224, 256), 1)
    sel[...] = (c == lax.rem(r, 32) * 8 + r // 32).astype(BF)
    r, c = iota((256, 224), 0), iota((256, 224), 1)
    pack[...] = (r == lax.rem(c, 32) * 8 + c // 32).astype(BF)
    lower = (iota((TOK, TOK), 0) > iota((TOK, TOK), 1)).astype(BF)
    eye = (iota((TOK, TOK), 0) == iota((TOK, TOK), 1)).astype(BF)
    gates_own[...] = jnp.zeros_like(gates_own)
    rk_own[...] = jnp.zeros_like(rk_own)

    def named(step):
        direction = jnp.where(s < 2, step, 1 - step)
        pair = routes_ref[direction]
        number = iota((EXPERTS, TOK), 0)
        names = jnp.logical_or(pair[0:1] == number, pair[1:2] == number)
        return names.astype(F32).astype(BF)

    for step in range(2):
        names = named(step)
        rank = nt(lower, names)
        kept = jnp.logical_and(nt(eye, names) > 0.5, rank < caps_ref[...].astype(F32))
        rk_own[step, :, 0:EXPERTS] = jnp.where(kept, rank, LOST).astype(BF)

    @pl.when(outer)
    def _():
        u_buf[0] = batches_ref[order_ref[jnp.where(s == 0, 0, 1)]]

    pl.semaphore_wait(barrier, 11)
    for p in range(2):
        send(rk_own, rk_near.at[p], rk_send, rk_recv, chip(0, 0, toward[p]))

    def layer(step, carry):
        direction = jnp.where(s < 2, step, 1 - step)

        def packer(ranks):
            rt = nt(onehot[...], ranks)
            main = (rt == lax.rem(iota((128, TOK), 0), 16).astype(F32)).astype(BF)
            rt7 = nt(onehot[...], jnp.concatenate([ranks] * NBLK, axis=0))
            rw, cl = iota((128, TOK * NBLK), 0), iota((128, TOK * NBLK), 1)
            want = (16 + lax.rem(rw, 16) // 8).astype(F32)
            ext = jnp.logical_and(rt7 == want, lax.rem(rw, 8) == cl // TOK).astype(BF)
            return main, ext

        pick_main[0], pick_ext[0] = packer(rk_own[step])

        def tables_near(p, carry):
            pick_main[p + 1], pick_ext[p + 1] = packer(rk_near[p, step])
            return carry

        first = jnp.logical_and(step == 0, outer)

        @pl.when(jnp.logical_and(step == 0, jnp.logical_not(outer)))
        def _():
            got(rk_near, rk_recv)

        @pl.when(jnp.logical_not(first))
        def _():
            lax.fori_loop(0, 2, tables_near, 0)

        @pl.when(jnp.logical_not(jnp.logical_and(step == 0, outer)))
        def _():
            got(u_buf.at[step], u_recv.at[step])

        total = jnp.zeros((TOK, 512), F32)
        for i in range(D // 512):
            v = u_buf[step, :, i * 512:(i + 1) * 512].astype(F32)
            total = total + v * v
        inv = lax.rsqrt(jnp.sum(total, axis=1, keepdims=True) * (1.0 / D) + 1e-06)
        for p in range(2):
            for i in range(p * HALF, (p + 1) * HALF, 256):
                v = u_buf[step, :, i:i + 256].astype(F32)
                normed[:, i:i + 256] = (v * inv * gain_ref[:, i:i + 256]).astype(BF)
            send(
                normed.at[:, p * HALF:(p + 1) * HALF], nb.at[step, p],
                nb_send, nb_recv.at[step, p], chip(0, 0, toward[p]),
            )

        def packed(which, source, put):
            main, ext = pick_main[which], pick_ext[which]
            for i in range(NBLK):
                put(i * BLK, mm(main, source(i)).astype(BF))
            stack = jnp.concatenate([source(i) for i in range(NBLK)], axis=0)
            put(HALF, mm(ext, stack).astype(BF))

        def send_own(i):
            (dx, dz), ch, j = offs[i], i // 4, i % 4
            for p in range(2):
                send(
                    sa.at[i - 1, :, lanes(p)], x_buf.at[step, ch, j * 16:j * 16 + 16, lanes(p)],
                    a1_send, a1_recv.at[step, p * 8 + i], chip(dx, dz, 0),
                )

        def send_near(p, i):
            (dx, dz), ch, at = offs[i], i // 4, near[p] * 64 + i % 4 * 16
            send(
                sb.at[p, i - 1], x_buf.at[step, ch, at:at + 16, lanes(p)],
                b_send, b_recv.at[step, p * 8 + i], chip(dx, dz, 0),
            )

        def forward_own(i):
            ch, j = i // 4, i % 4
            for p in range(2):
                at = toward[p] * 64 + j * 16
                if i:
                    got(x_buf.at[step, ch, j * 16:j * 16 + 16, lanes(p)], a1_recv.at[step, p * 8 + i])
                send(
                    x_buf.at[step, ch, j * 16:j * 16 + 16, lanes(p)], x_buf.at[step, ch, at:at + 16, lanes(p)],
                    a2_send, a2_recv.at[step, ch], chip(0, 0, near[p]),
                )

        def forward_near(p, i):
            ch, j = i // 4, i % 4
            at, to = near[p] * 64 + j * 16, 128 + j * 16
            if i:
                got(x_buf.at[step, ch, at:at + 16, lanes(p)], b_recv.at[step, p * 8 + i])
            send(
                x_buf.at[step, ch, at:at + 16, lanes(p)], x_buf.at[step, ch, to:to + 16, lanes(p)],
                a2_send, a2_recv.at[step, ch], chip(0, 0, toward[p]),
            )

        for p in range(2):
            def put_own(at, v):
                x_buf[step, 0, 0:16, p * WIDE + at:p * WIDE + at + BLK] = v[0:16]
                sa[:, :, p * WIDE + at:p * WIDE + at + BLK] = v[16:128].reshape(7, 16, BLK)

            packed(0, lambda i: normed[:, p * HALF + i * BLK:p * HALF + (i + 1) * BLK], put_own)
        for i in range(1, 8):
            send_own(i)
        forward_own(0)

        router = router_ref[...]
        high = router.astype(BF)
        low = (router - high.astype(F32)).astype(BF)
        scores = jax.nn.sigmoid(nt(normed[...], high) + nt(normed[...], low))
        chosen = jnp.sum(nt(eye, named(step)) * scores, axis=1, keepdims=True)
        gates_own[step, :, 0:EXPERTS] = (2.5 * scores / chosen).astype(BF)
        for p in range(2):
            send(gates_own.at[step], gates_near.at[step, p], g_send, g_recv.at[step], chip(0, 0, toward[p]))

        @pl.when(first)
        def _():
            got(rk_near, rk_recv)
            lax.fori_loop(0, 2, tables_near, 0)

        for p in range(2):
            def put_near(at, v):
                at_row = near[p] * 64
                x_buf[step, 0, at_row:at_row + 16, p * WIDE + at:p * WIDE + at + BLK] = v[0:16]
                sb[p, :, :, at:at + BLK] = v[16:128].reshape(7, 16, BLK)

            got(nb.at[step, p], nb_recv.at[step, p])
            packed(p + 1, lambda i: nb[step, p, :, i * BLK:(i + 1) * BLK], put_near)
            for i in (1, 2, 3):
                send_near(p, i)
            forward_near(p, 0)
        for i in range(4, 8):
            for p in range(2):
                send_near(p, i)
        for i in range(1, 8):
            forward_own(i)

        for p in range(2):
            for i in (1, 2, 3):
                forward_near(p, i)
        for i in range(4, 8):
            for p in range(2):
                forward_near(p, i)

        @pl.when(step == 0)
        def _():
            copy_in.wait()
            copy_down.wait()

        def arrived(ch):
            got(x_buf.at[step, ch, 0:ROWS, 0:WIDE], a2_recv.at[step, ch])
            for p in range(2):
                spread = mm(sel[...], x_buf[step, ch, 0:ROWS, p * WIDE + HALF:(p + 1) * WIDE]).astype(BF)
                for i in range(NBLK):
                    cols = slice(p * WIDE + i * BLK, p * WIDE + (i + 1) * BLK)
                    x_buf[step, ch, ROWS:XROWS, cols] = spread[i * 32:(i + 1) * 32]

        def up(ch, n):
            cols = slice(n * 256, (n + 1) * 256)
            g, v = (
                mm(x_buf[step, ch, :, 0:HALF], w_in[q, 0:HALF, cols])
                + mm(x_buf[step, ch, :, WIDE:WIDE + HALF], w_in[q, HALF:D, cols])
                for q in range(2)
            )
            hidden[:, cols] = (jax.nn.silu(g) * v).astype(BF)

        def down(ch, p):
            for n in range(NBLK):
                v = mm(hidden[...], w_down[:, p * HALF + n * BLK:p * HALF + (n + 1) * BLK]).astype(BF)
                out_buf[ch, 0:ROWS, p * WIDE + n * BLK:p * WIDE + (n + 1) * BLK] = v[0:ROWS]
                ext_out[n * 32:(n + 1) * 32, :] = v[ROWS:XROWS]
            out_buf[ch, 0:ROWS, p * WIDE + HALF:(p + 1) * WIDE] = mm(pack[...], ext_out[...]).astype(BF)

        def send_part(ch, p, q):
            first, to = (128, near[p]) if q else (toward[p] * 64, toward[p])
            send(
                out_buf.at[ch, first:first + 64, lanes(p)], part.at[step, ch, p * 2 + q],
                part_send, part_recv.at[step, ch * 4 + p * 2 + q], chip(0, 0, to),
            )

        def back(ch, p, q):
            got(part.at[step, ch, p * 2 + q], part_recv.at[step, ch * 4 + p * 2 + q])
            for j in range(4):
                i = ch * 4 + j
                dx, dz = offs[i]
                first = near[p] * 64 * q + j * 16
                v = out_buf[ch, first:first + 16, lanes(p)].astype(F32)
                v = (v + part[step, ch, p * 2 + q, j * 16:j * 16 + 16].astype(F32)).astype(BF)
                if q and i:
                    sn2[p, i - 1] = v
                    send(sn2.at[p, i - 1], rn2.at[step, p, i], rn2_send, rn2_recv.at[step, p], chip(dx, -dz, 0))
                elif q:
                    rn2[step, p, 0] = v
                elif i:
                    sa2[i - 1, :, lanes(p)] = v
                    if ch or p:
                        cut = lanes(p) if ch else slice(0, 2 * WIDE)
                        send(
                            sa2.at[i - 1, :, cut], ra2.at[step, i, :, cut],
                            ra2_send, ra2_recv.at[step, ch * p], chip(dx, -dz, 0),
                        )
                else:
                    ra2[step, 0, :, lanes(p)] = v

        def weights(ranks, gate):
            rt, gt = nt(ranks, onehot[...]), nt(gate, onehot[...])
            main = jnp.where(rt == lax.rem(iota((TOK, 128), 1), 16).astype(F32), gt, 0.0).astype(BF)
            rw, cl = iota((TOK * NBLK, 128), 0), iota((TOK * NBLK, 128), 1)
            want = (16 + lax.rem(cl, 16) // 8).astype(F32)
            take = jnp.logical_and(
                jnp.concatenate([rt] * NBLK, axis=0) == want, lax.rem(cl, 8) == rw // TOK
            )
            return main, jnp.where(take, jnp.concatenate([gt] * NBLK, axis=0), 0.0).astype(BF)

        got(gates_near.at[step], g_recv.at[step])
        for p in range(2):
            gate_main[p], gate_ext[p] = weights(rk_near[p, step], gates_near[step, p])
        gate_main[2], gate_ext[2] = weights(rk_own[step], gates_own[step])

        arrived(0)
        up(0, 0)
        up(0, 1)
        for p in range(2):
            down(0, p)
            send_part(0, p, 1)
            send_part(0, p, 0)
        arrived(1)
        up(1, 0)
        up(1, 1)
        down(1, 0)
        send_part(1, 0, 1)
        down(1, 1)
        send_part(1, 1, 1)
        back(0, 0, 1)
        back(0, 1, 1)
        send_part(1, 0, 0)
        send_part(1, 1, 0)
        back(0, 0, 0)
        back(0, 1, 0)
        for q in (1, 0):
            for p in range(2):
                back(1, p, q)

        def weighed(tables, source, put):
            main, ext = tables
            over = mm(ext, source(HALF))
            for i in range(NBLK):
                put(i * BLK, mm(main, source(i * BLK)) + over[i * TOK:(i + 1) * TOK])

        cuts = slice(0, 4 * BLK), slice(4 * BLK, HALF)

        for p in range(2):
            def put_back(at, v):
                s3[p, :, at:at + BLK] = v.astype(BF)

            tables = gate_main[p], gate_ext[p]
            got(rn2.at[step, p, 1:8], rn2_recv.at[step, p])
            weighed(tables, lambda at: rn2[step, p, :, :, at:at + BLK].reshape(128, BLK), put_back)
            for h, cut in enumerate(cuts):
                send(s3.at[p, :, cut], r3.at[step, p, :, cut], r3_send, r3_recv.at[step, p * 2 + h], chip(0, 0, near[p]))

        tables = gate_main[2], gate_ext[2]
        rows_first = ra2.at[step, 0:5]
        for p in range(2):
            if p == 0:
                got(rows_first, ra2_recv.at[step, 0])
            else:
                got(ra2.at[step, 4:8, :, lanes(1)], ra2_recv.at[step, 1])

            def put_sum(at, v):
                cols = slice(p * HALF + at, p * HALF + at + BLK)
                total_out[:, cols] = u_buf[step, :, cols].astype(F32) + v

            weighed(tables, lambda at: ra2[step, :, :, p * WIDE + at:p * WIDE + at + BLK].reshape(128, BLK), put_sum)

        target = jnp.where(direction == 0, s + 1, s - 1)
        relays = jnp.logical_and(target >= 0, target <= 3)
        target_step = jnp.where(jnp.logical_and(step == 0, outer), 0, 1)
        for h, cut in enumerate(cuts):
            for p in range(2):
                got(r3.at[step, p, :, cut], r3_recv.at[step, p * 2 + h])
                for at in range(cut.start, cut.stop, BLK):
                    cols = slice(p * HALF + at, p * HALF + at + BLK)
                    v = total_out[:, cols] + r3[step, p, :, at:at + BLK].astype(F32)
                    out_ref[direction, :, cols] = v.astype(BF)
                half = slice(p * HALF + cut.start, p * HALF + cut.stop)

                @pl.when(relays)
                def _():
                    send(
                        out_ref.at[direction, :, half], u_buf.at[target_step, :, half],
                        u_send, u_recv.at[target_step], (target, me),
                    )

        sent(nb.at[step], nb_send)
        sent(sa, a1_send)
        sent(sb, b_send)
        sent(x_buf.at[step, :, 0:ROWS, 0:WIDE], a2_send)
        sent(gates_near.at[step], g_send)
        sent(part.at[step], part_send)
        sent(sa2, ra2_send)
        sent(sn2, rn2_send)
        sent(s3, r3_send)

        @pl.when(relays)
        def _():
            sent(u_buf.at[step], u_send)

        return carry

    lax.fori_loop(0, 2, layer, 0)
    sent(rk_near, rk_send)


def local(batches, order, gains, router, routes, caps, w_in, w_down):
    vmem, hbm = pl.BlockSpec(memory_space=pltpu.VMEM), pl.BlockSpec(memory_space=pl.ANY)
    dma = pltpu.SemaphoreType.DMA
    out = pl.pallas_call(
        kernel,
        out_shape=jax.ShapeDtypeStruct((2, TOK, D), BF),
        in_specs=[pl.BlockSpec(memory_space=pltpu.SMEM), vmem, vmem, vmem, vmem, vmem, hbm, hbm],
        out_specs=vmem,
        scratch_shapes=[
            pltpu.VMEM((2, D, HID), BF),
            pltpu.VMEM((HID, D), BF),
            pltpu.VMEM((2, TOK, D), BF),
            pltpu.VMEM((TOK, D), BF),
            pltpu.VMEM((128, 128), BF),
            pltpu.VMEM((2, TOK, 128), BF),
            pltpu.VMEM((2, 2, TOK, 128), BF),
            pltpu.VMEM((2, TOK, 128), BF),
            pltpu.VMEM((2, 2, TOK, 128), BF),
            pltpu.VMEM((3, 128, TOK), BF),
            pltpu.VMEM((3, 128, TOK * NBLK), BF),
            pltpu.VMEM((224, 256), BF),
            pltpu.VMEM((256, 224), BF),
            pltpu.VMEM((2, 2, TOK, HALF), BF),
            pltpu.VMEM((2, 2, XROWS, 2 * WIDE), BF),
            pltpu.VMEM((7, 16, 2 * WIDE), BF),
            pltpu.VMEM((2, 7, 16, WIDE), BF),
            pltpu.VMEM((XROWS, HID), BF),
            pltpu.VMEM((224, 256), BF),
            pltpu.VMEM((2, ROWS, 2 * WIDE), BF),
            pltpu.VMEM((2, 2, 4, 64, WIDE), BF),
            pltpu.VMEM((7, 16, 2 * WIDE), BF),
            pltpu.VMEM((2, 7, 16, WIDE), BF),
            pltpu.VMEM((2, 8, 16, 2 * WIDE), BF),
            pltpu.VMEM((2, 2, 8, 16, WIDE), BF),
            pltpu.VMEM((2, TOK, HALF), BF),
            pltpu.VMEM((2, 2, TOK, HALF), BF),
            pltpu.VMEM((TOK, D), F32),
            pltpu.VMEM((3, TOK, 128), BF),
            pltpu.VMEM((3, TOK * NBLK, 128), BF),
            dma((2,)),
            dma, dma,
            dma, dma((2,)),
            dma, dma((2, 2)),
            dma, dma((2, 16)),
            dma, dma((2, 16)),
            dma, dma((2, 2)),
            dma, dma((2, 8)),
            dma, dma((2, 2)),
            dma, dma((2, 2)),
            dma, dma((2, 4)),
            dma, dma((2,)),
        ],
        compiler_params=pltpu.CompilerParams(
            collective_id=0, has_side_effects=True, vmem_limit_bytes=60 << 20
        ),
        name="relay",
    )(order, batches, gains, router[0].T, jnp.swapaxes(routes[0], 1, 2), caps, w_in[0], w_down[0])
    return out[None]


def solution(mesh):
    placed = (
        P(None, "expert", None),
        P(),
        P("section", None),
        P("section", None, None),
        P("section", None, "expert", None),
        P("section", None),
        P("section", None, None, "expert"),
        P("section", "expert", None),
    )
    return jax.shard_map(
        local,
        mesh=mesh,
        in_specs=placed,
        out_specs=P("section", None, "expert", None),
        check_vma=False,
    )
```
